256 devices in a mesh: db: 16 (over y, x), seq: 8 (over z), batch: 2 (over core).
Axes of the slice: x: 4, y: 4, z: 8, core: 2. Of those that a mesh axis runs over, the one named last changes fastest.
Arguments:
- queries: bfloat16 [32, 1024, 2048], P(('db', 'batch'), 'seq'), may hold values from -26 to 26
- database: bfloat16 [128, 128, 896], P('db'), may hold values from -100 to 100
- enc_gain: float32 [896], replicated, may hold values from 0.1 to 1.9
- kv_weight: bfloat16 [2, 896, 2048], replicated, as said below
- shard_ids: int32 [32, 16, 2, 1], P(('db', 'batch'), 'seq'), may hold values from 0 to 15; in each aligned block of 4 rows (0 to 3, 4 to 7, ..., all dimensions but the last counted through in order) at most 2 rows name the same one
- block_ids: int32 [32, 16, 2], P(('db', 'batch'), 'seq'), may hold values from 0 to 7
Outputs:
- attended: bfloat16 [32, 1024, 2048], P(('db', 'batch'), 'seq')
The draws below stay inside these ranges and needn't reach their ends.
Inputs may be any that keep to these rules, and one draw needn't show every extreme that they name: `shard_ids`: among the neighbours of the rows of one device (one aligned block of 4 neighbours) at most 2 name the same shard. `kv_weight`: entries of order 896 ** -0.5.
All inputs are finite; a program needn't handle non-finite values.
Results may differ from the reference program's by a relative error of at most 0.012.
Values may be sent and summed in bfloat16 or wider, within the bound.
No kernel may reach another device: no remote copies, remote signals or barrier semaphores. Data moves between devices by JAX's collectives and lax.ppermute only.
A program may use at most 192 MiB of HBM per device.

```python
import math
import jax
import jax.numpy as jnp
import numpy as np
from jax import lax

D = 2048
HEADS = 16
DE = 896
SPAN = 64
NBRS = 2
NBR_LEN = 128
TOK_DEV = 128
CAP = 2
BLK_SHARD = 8
LEN = 1024
SPANS = 16
SEQS = 32
DB_BLOCKS = 128
N_DB = 16


def kv_tables(key):
    return jax.random.normal(jax.random.fold_in(key, 11), (2, DE, D), jnp.float32) * DE ** (-0.5)


def draw_kv_weight(key, part):
    return kv_tables(key).astype(jnp.bfloat16)


def draw_database(key, part):
    base_key, row_key, column_key = jax.random.split(jax.random.fold_in(key, 13), 3)
    full_shape = (DB_BLOCKS, NBR_LEN, DE)
    row_scale = jnp.exp(jax.random.uniform(row_key, (DB_BLOCKS, NBR_LEN, 1), jnp.float32) * math.log(10.0))
    column_scale = jnp.exp(jax.random.uniform(column_key, (1, 1, DE), jnp.float32) * math.log(10.0))
    drawn = jnp.clip(jax.random.normal(base_key, full_shape, jnp.float32) * 0.4, -1.0, 1.0)
    entries = drawn * row_scale * column_scale
    return entries.astype(jnp.bfloat16)


def draw_queries(key, part):
    full_shape = (SEQS, LEN, D)
    base_key = jax.random.fold_in(key, 14)
    drawn = jnp.clip(jax.random.normal(base_key, full_shape, jnp.float32) * 2.0, -8.0, 8.0)
    return drawn.astype(jnp.bfloat16)


def set_ends(values, rng, smallest, top_value):
    longest = values.shape.index(max(values.shape))
    spots = []
    for shift in (0, 1):
        where = [jax.random.randint(jax.random.fold_in(rng, axis), (), 0, length) for axis, length in enumerate(values.shape)]
        where[longest] = (where[longest] + shift) % values.shape[longest]
        spots.append(tuple(where))
    return values.at[spots[0]].set(smallest).at[spots[1]].set(top_value)


def routed_block(own_key, own, number, rows, number_of, top, bound, slope):
    ranking = jax.random.permutation(own_key, number_of)
    crowded, common = portions_of(number_of, rows * top, bound, slope, True), portions_of(number_of, rows * top, bound, slope, False)
    places = jnp.arange(number_of)

    def named(lengths, offset_by):
        used = int((lengths > 0).sum())
        fixed = max(1, used // 4)
        moved = fixed + (places - fixed + offset_by * (used - fixed)) % max(1, number_of - fixed)
        return jnp.zeros((number_of,), jnp.int32).at[ranking[jnp.where(places < fixed, places, moved)]].set(jnp.asarray(lengths, jnp.int32))

    lengths = jnp.where(number % 4 == 0, named(crowded, number // 4), named(common, number - number // 4 - 1))
    mixed = jax.random.permutation(jax.random.fold_in(own, 3), number_of)
    giver, taker = mixed[0:number_of // 2 * 2:2], mixed[1:number_of // 2 * 2:2]
    margin = jnp.minimum(lengths[giver] - 1, bound - lengths[taker]) // 2
    margin = jnp.where((giver == ranking[0]) | (taker == ranking[0]) | (lengths[taker] == 0), 0, jnp.maximum(margin, 0))
    moved = jax.random.randint(jax.random.fold_in(own, 4), (number_of // 2,), 0, 1 << 20) % (margin + 1)
    lengths = lengths.at[giver].add(-moved).at[taker].add(moved)
    members = jnp.searchsorted(jnp.cumsum(lengths), jnp.arange(rows * top), side="right").astype(jnp.int32)
    grid = members.reshape(top, rows).T
    grid = grid[jax.random.permutation(jax.random.fold_in(own, 1), rows)]
    offset_by = jax.random.randint(jax.random.fold_in(own, 2), (rows, 1), 0, top)
    return jnp.take_along_axis(grid, (jnp.arange(top)[None, :] + offset_by) % top, axis=1)


def portions_of(amount, total, bound, slope, full):
    weights = [(1 << 20) // math.isqrt(rank ** slope) + 1 for rank in range(1, amount + 1)]
    largest = bound if full else min(bound, max(-(-total // amount), total * weights[0] // sum(weights)))
    least = 1 if total - largest >= amount - 1 else 0
    counts, rest = [largest] + [least] * (amount - 1), total - largest - least * (amount - 1)
    while rest > 0:
        free = [i for i in range(1, amount) if counts[i] < largest] or [i for i in range(1, amount) if counts[i] < bound]
        whole, budget = sum([weights[i] for i in free]), rest
        for i in free:
            more = min(bound - counts[i], max(1, budget * weights[i] // whole), rest)
            counts[i] = counts[i] + more
            rest = rest - more
    return np.array(counts)


def setup_inputs(seed: int = 0) -> dict:
    keys = jax.random.split(jax.random.key(seed), 7)
    queries = draw_queries(jax.random.fold_in(keys[6], 71), 0)
    database = draw_database(jax.random.fold_in(keys[6], 71), 0)
    enc_gain = jnp.clip(1.0 + 0.18 * jax.random.normal(keys[2], (DE,), jnp.float32), 0.1, 1.9)
    kv_weight = draw_kv_weight(jax.random.fold_in(keys[6], 71), 0)
    shard_ids_keys = jax.random.split(jax.random.fold_in(keys[4], 1), SEQS * SPANS * NBRS // (TOK_DEV // SPAN * NBRS))
    shard_ids_turns = jax.random.permutation(jax.random.fold_in(keys[4], 3), SEQS * SPANS * NBRS // (TOK_DEV // SPAN * NBRS))
    shard_ids = jax.vmap(lambda own, number: routed_block(jax.random.fold_in(keys[4], 2), own, number, TOK_DEV // SPAN * NBRS, N_DB, 1, CAP, 2))(shard_ids_keys, shard_ids_turns).reshape((SEQS, SPANS, NBRS, 1))
    block_ids = set_ends(jax.random.randint(keys[5], (SEQS, SPANS, NBRS), 0, BLK_SHARD), jax.random.fold_in(keys[5], 1), 0, BLK_SHARD - 1).astype(jnp.int32)
    return {"queries": queries, "database": database, "enc_gain": enc_gain, "kv_weight": kv_weight, "shard_ids": shard_ids, "block_ids": block_ids}


epsilon = 1e-06

def encode(blocks, enc_gain, kv_weight):
    flattened = blocks.reshape(-1, blocks.shape[-1]).astype(jnp.float32)
    factor = lax.rsqrt(lax.optimization_barrier(jnp.mean(flattened * flattened, axis=1, keepdims=True)) + epsilon)
    normed = (flattened * factor * enc_gain).astype(jnp.bfloat16)
    key_rows = jnp.dot(normed, kv_weight[0], preferred_element_type=jnp.float32).astype(jnp.bfloat16)
    value_rows = jnp.dot(normed, kv_weight[1], preferred_element_type=jnp.float32).astype(jnp.bfloat16)
    return (key_rows.reshape(blocks.shape[:-1] + (key_rows.shape[-1],)), value_rows.reshape(blocks.shape[:-1] + (value_rows.shape[-1],)))

def attend(query_groups, key_groups, value_groups):
    group_count, group_rows, model_width = query_groups.shape
    head_dim = model_width // HEADS
    query_heads = query_groups.astype(jnp.float32).reshape(group_count, group_rows, HEADS, head_dim)
    key_heads = key_groups.astype(jnp.float32).reshape(group_count, -1, HEADS, head_dim)
    value_heads = value_groups.astype(jnp.float32).reshape(group_count, -1, HEADS, head_dim)
    scores = jnp.einsum('gqhd,gkhd->ghqk', query_heads, key_heads, precision=lax.Precision.HIGHEST) * head_dim ** (-0.5)
    highest = lax.optimization_barrier(jnp.max(scores, axis=-1, keepdims=True))
    raised = jnp.exp(scores - highest)
    weights = (raised / lax.optimization_barrier(jnp.sum(raised, axis=-1, keepdims=True))).astype(jnp.bfloat16)
    weights = lax.optimization_barrier(weights)
    mixture = jnp.einsum('ghqk,gkhd->gqhd', weights.astype(jnp.float32), value_heads, precision=lax.Precision.HIGHEST)
    return mixture.reshape(group_count, group_rows, model_width).astype(jnp.bfloat16)

def reference(queries, database, enc_gain, kv_weight, shard_ids, block_ids):
    key_rows, value_rows = encode(database, enc_gain, kv_weight)
    key_rows, value_rows = lax.optimization_barrier((key_rows, value_rows))
    offset_rows = SPAN - 1

    def one_sequence(operands):
        sequence, shards, blocks = operands
        indices = (shards[:, :, 0] * BLK_SHARD + blocks).reshape(-1).astype(jnp.int32)
        chosen_keys = jnp.take(key_rows, indices, axis=0).reshape(SPANS, NBRS * NBR_LEN, D)
        chosen_values = jnp.take(value_rows, indices, axis=0).reshape(SPANS, NBRS * NBR_LEN, D)
        shifted = jnp.concatenate([sequence[offset_rows:], jnp.zeros((offset_rows, D), sequence.dtype)], axis=0)
        mixture = attend(shifted.reshape(SPANS, SPAN, D), chosen_keys, chosen_values).reshape(LEN, D)
        return jnp.concatenate([jnp.zeros((offset_rows, D), mixture.dtype), mixture[:LEN - offset_rows]], axis=0)
    return lax.map(one_sequence, (queries, shard_ids, block_ids))
```

```python
import jax
import jax.numpy as jnp
from jax import lax
from jax.experimental import pallas as pl
from jax.experimental.pallas import tpu as pltpu
from jax.sharding import PartitionSpec as P

HEADS = 16
SPAN = 64
NBRS = 2
EPS = 1e-06
COLUMN = ("seq", "batch")
TILE = 256


def ring(value, axis, steps):
    count = lax.axis_size(axis)
    return lax.ppermute(value, axis, [(i, (i + steps) % count) for i in range(count)])


def normed_slice(database, enc_gain, part, parts):
    rows = database.shape[1] // parts
    own = lax.dynamic_slice_in_dim(database, part * rows, rows, axis=1).astype(jnp.float32)
    factor = lax.rsqrt(jnp.mean(own * own, axis=-1, keepdims=True) + EPS)
    return (own * factor * enc_gain).astype(jnp.bfloat16)


def pick_kernel(ids_ref, rows_ref, first_ref, second_ref):
    count = first_ref.shape[0]

    def step(i, carry):
        first_ref[i] = rows_ref[ids_ref[i]]
        second_ref[i] = rows_ref[ids_ref[count + i]]
        return carry

    lax.fori_loop(0, count, step, 0, unroll=8)


def pick(ids, rows):
    count = ids.shape[0] // 2
    shape = jax.ShapeDtypeStruct((count,) + rows.shape[1:], rows.dtype)
    return pl.pallas_call(
        pick_kernel,
        out_shape=(shape, shape),
        in_specs=[
            pl.BlockSpec(memory_space=pltpu.SMEM),
            pl.BlockSpec(memory_space=pltpu.VMEM),
        ],
        out_specs=(pl.BlockSpec(memory_space=pltpu.VMEM), pl.BlockSpec(memory_space=pltpu.VMEM)),
        name="pick",
    )(ids, rows)


def attend_kernel(rows_ref, weight_ref, query_ref, out_ref):
    width = query_ref.shape[1]
    head = width // HEADS
    rows = rows_ref[...]
    for start in range(0, width, TILE):
        columns = slice(start, start + TILE)
        keys = jnp.dot(rows, weight_ref[0, :, columns], preferred_element_type=jnp.float32)
        values = jnp.dot(rows, weight_ref[1, :, columns], preferred_element_type=jnp.float32)
        keys = keys.astype(jnp.bfloat16)
        values = values.astype(jnp.bfloat16)
        for inner in range(0, TILE, head):
            own = slice(start + inner, start + inner + head)
            part = slice(inner, inner + head)
            scores = lax.dot_general(
                query_ref[:, own],
                keys[:, part],
                (((1,), (1,)), ((), ())),
                preferred_element_type=jnp.float32,
            ) * head ** (-0.5)
            raised = jnp.exp(scores - jnp.max(scores, axis=-1, keepdims=True))
            weights = (raised / jnp.sum(raised, axis=-1, keepdims=True)).astype(jnp.bfloat16)
            mixed = jnp.dot(weights, values[:, part], preferred_element_type=jnp.float32)
            out_ref[:, own] = mixed.astype(out_ref.dtype)


def attend(rows, kv_weight, queries):
    vmem = pl.BlockSpec(memory_space=pltpu.VMEM)
    flops = 2 * rows.shape[0] * kv_weight.shape[1] * kv_weight.shape[2] * 2
    return pl.pallas_call(
        attend_kernel,
        out_shape=jax.ShapeDtypeStruct(queries.shape, queries.dtype),
        in_specs=[vmem] * 3,
        out_specs=vmem,
        compiler_params=pltpu.CompilerParams(vmem_limit_bytes=32 * 2**20),
        cost_estimate=pl.CostEstimate(flops=flops, bytes_accessed=2**20, transcendentals=2**18),
        name="attend",
    )(rows, kv_weight, queries)


def body(queries, database, enc_gain, kv_weight, shard_ids, block_ids):
    own = queries[0]
    tokens, width = own.shape
    seq, cores = lax.axis_size("seq"), lax.axis_size("batch")
    place = lax.axis_index("seq")
    parts = seq * cores
    slab = normed_slice(database, enc_gain, lax.axis_index(COLUMN), parts)
    slabs = lax.all_gather(slab, "db", axis=0, tiled=True)
    wanted = (shard_ids[..., 0] * database.shape[0] + block_ids).reshape(1, 2, NBRS)
    wanted = lax.all_gather(wanted, COLUMN, axis=0, tiled=True).reshape(seq, cores, 2, NBRS)
    prior = jnp.roll(wanted[:, :, 1], 1, axis=0)
    ids = jnp.stack([prior, wanted[:, :, 0]]).reshape(-1)
    sent = pick(ids, slabs)
    rows = []
    for chosen in sent:
        chosen = chosen.reshape((parts, NBRS) + chosen.shape[1:])
        arrived = lax.all_to_all(chosen, COLUMN, split_axis=0, concat_axis=0, tiled=True)
        rows.append(arrived.reshape(-1, arrived.shape[-1]))
    last = ring(own[tokens - 1 :], "seq", 1)
    prior_queries = jnp.concatenate([own[: SPAN - 1], last])
    own_queries = jnp.concatenate([own[SPAN : tokens - 1], own[SPAN - 1 : SPAN]])
    prior_out = attend(rows[0], kv_weight, prior_queries)
    back = ring(prior_out[SPAN - 1 :], "seq", -1)
    own_out = attend(rows[1], kv_weight, own_queries)
    head = jnp.where(place == 0, jnp.zeros_like(prior_out), prior_out)[: SPAN - 1]
    result = jnp.concatenate([head, own_out[SPAN - 1 :], own_out[: SPAN - 1], back])
    return result[None]


def solution(mesh):
    in_specs = (
        P(("db", "batch"), "seq", None),
        P("db", None, None),
        P(),
        P(),
        P(("db", "batch"), "seq", None, None),
        P(("db", "batch"), "seq", None),
    )
    out_specs = P(("db", "batch"), "seq", None)
    return jax.shard_map(body, mesh=mesh, in_specs=in_specs, out_specs=out_specs, check_vma=False)
```

```python
import jax
import jax.numpy as jnp
from jax import lax
from jax.experimental import pallas as pl
from jax.experimental.pallas import tpu as pltpu
from jax.sharding import PartitionSpec as P

HEADS = 16
SPAN = 64
NBRS = 2
EPS = 1e-06
COLUMN = ("seq", "batch")
PLANE = ("db", "batch")
SIDE = 4
TILE = 256


def ring(value, axis, steps):
    count = lax.axis_size(axis)
    return lax.ppermute(value, axis, [(i, (i + steps) % count) for i in range(count)])


def shifted(place, along_x, steps):
    y, x = divmod(place, SIDE)
    return y * SIDE + (x + steps) % SIDE if along_x else (y + steps) % SIDE * SIDE + x


def plane_shift(value, stage, steps):
    pairs = []
    for place in range(lax.axis_size("db")):
        for core in range(lax.axis_size("batch")):
            goal = shifted(place, (core + stage) % 2 == 0, steps)
            pairs.append((place * 2 + core, goal * 2 + core))
    return lax.ppermute(value, PLANE, pairs)


def plane_gather(slab):
    first = {steps: plane_shift(slab, 0, steps) for steps in (1, 3, 2)}
    first = jnp.stack([slab] + [first[steps] for steps in (1, 2, 3)])
    second = {steps: plane_shift(first, 1, steps) for steps in (1, 3, 2)}
    return [first] + [second[steps] for steps in (1, 2, 3)]


def pick_kernel(place_ref, wanted_ref, *refs):
    pieces, out_ref, held_ref, sems = refs[:-3], refs[-3], refs[-2], refs[-1]
    count, slots = out_ref.shape[:2]
    cores = 2
    blocks = pieces[0].shape[0] // SIDE
    x, y, core = place_ref[0], place_ref[1], place_ref[2]

    def one(goal, slot, code):
        shard, block = code // blocks, code % blocks
        back_x = (x - shard % SIDE + SIDE) % SIDE
        back_y = (y - shard // SIDE + SIDE) % SIDE
        inner = jnp.where(core == 0, back_x, back_y)
        outer = jnp.where(core == 0, back_y, back_x)
        where = inner * blocks + block
        value = pieces[0][where]
        for step in range(1, SIDE):
            value = jnp.where(outer == step, pieces[step][where], value)
        held_ref[goal, slot] = value

    def send(goal):
        return pltpu.make_async_copy(held_ref.at[goal], out_ref.at[goal], sems.at[goal])

    def step(goal, carry):
        before = lax.rem(goal + count - cores, count)
        for slot in range(NBRS):
            one(goal, slot, wanted_ref[before * slots + NBRS + slot])
            one(goal, NBRS + slot, wanted_ref[goal * slots + slot])
        send(goal).start()
        return carry

    lax.fori_loop(0, count, step, 0, unroll=4)
    for goal in range(count):
        send(goal).wait()


def pick(place, wanted, pieces, count, slots):
    vmem = pl.BlockSpec(memory_space=pltpu.VMEM)
    smem = pl.BlockSpec(memory_space=pltpu.SMEM)
    shape = (count, slots) + pieces[0].shape[1:]
    pieces = [pltpu.with_memory_space_constraint(piece, pltpu.VMEM) for piece in pieces]
    return pl.pallas_call(
        pick_kernel,
        out_shape=pltpu.HBM(shape, pieces[0].dtype),
        in_specs=[smem, smem] + [vmem] * len(pieces),
        out_specs=pl.BlockSpec(memory_space=pltpu.HBM),
        scratch_shapes=[pltpu.VMEM(shape, pieces[0].dtype), pltpu.SemaphoreType.DMA((count,))],
        compiler_params=pltpu.CompilerParams(vmem_limit_bytes=8 * 2**20),
        name="pick",
    )(place, wanted, *pieces)


def attend_kernel(rows_ref, gain_ref, weight_ref, query_ref, spare_ref, out_ref, normed_ref, held_ref, sems):
    width = query_ref.shape[1]
    head = width // HEADS
    tiles = width // TILE

    def load(tile):
        return pltpu.make_async_copy(
            weight_ref.at[:, :, pl.ds(tile * TILE, TILE)], held_ref.at[tile], sems.at[tile]
        )

    for tile in range(tiles):
        load(tile).start()
    raw = rows_ref[...].reshape(normed_ref.shape).astype(jnp.float32)
    factor = lax.rsqrt(jnp.mean(raw * raw, axis=-1, keepdims=True) + EPS)
    normed_ref[...] = (raw * factor * gain_ref[...]).astype(jnp.bfloat16)
    bottom = lax.broadcasted_iota(jnp.int32, (SPAN, head), 0) == SPAN - 1
    for tile in range(tiles):
        load(tile).wait()
        rows = normed_ref[...]
        keys = jnp.dot(rows, held_ref[tile, 0], preferred_element_type=jnp.float32)
        values = jnp.dot(rows, held_ref[tile, 1], preferred_element_type=jnp.float32)
        keys = keys.astype(jnp.bfloat16)
        values = values.astype(jnp.bfloat16)
        for inner in range(0, TILE, head):
            own = slice(tile * TILE + inner, tile * TILE + inner + head)
            part = slice(inner, inner + head)
            queries = jnp.where(
                bottom, spare_ref[:, own].astype(jnp.float32), query_ref[:, own].astype(jnp.float32)
            ).astype(jnp.bfloat16)
            scores = lax.dot_general(
                queries, keys[:, part], (((1,), (1,)), ((), ())), preferred_element_type=jnp.float32
            ) * head ** (-0.5)
            raised = jnp.exp(scores - jnp.max(scores, axis=-1, keepdims=True))
            weights = (raised / jnp.sum(raised, axis=-1, keepdims=True)).astype(jnp.bfloat16)
            mixed = jnp.dot(weights, values[:, part], preferred_element_type=jnp.float32)
            out_ref[:, own] = mixed.astype(out_ref.dtype)


def attend(span, rows, gain, kv_weight, queries, spare):
    parts, height, depth = rows.shape
    tokens, width = queries.shape
    whole = pl.BlockSpec(memory_space=pltpu.VMEM)
    tiles = width // TILE
    flops = 2 * 256 * depth * width * 2
    return pl.pallas_call(
        attend_kernel,
        grid=(1,),
        out_shape=jax.ShapeDtypeStruct((SPAN, width), queries.dtype),
        in_specs=[
            pl.BlockSpec((parts, height // 2, depth), lambda i: (0, span, 0)),
            whole,
            pl.BlockSpec(memory_space=pltpu.HBM),
            pl.BlockSpec((SPAN, width), lambda i: (span, 0)),
            whole,
        ],
        out_specs=pl.BlockSpec((SPAN, width), lambda i: (0, 0)),
        scratch_shapes=[
            pltpu.VMEM((parts * height // 2, depth), jnp.bfloat16),
            pltpu.VMEM((tiles, 2, depth, TILE), jnp.bfloat16),
            pltpu.SemaphoreType.DMA((tiles,)),
        ],
        compiler_params=pltpu.CompilerParams(vmem_limit_bytes=24 * 2**20),
        cost_estimate=pl.CostEstimate(flops=flops, bytes_accessed=2**23, transcendentals=2**18),
        name="attend",
    )(rows, gain, pltpu.with_memory_space_constraint(kv_weight, pltpu.HBM), queries, spare)


def body(queries, database, enc_gain, kv_weight, shard_ids, block_ids):
    own = queries[0]
    tokens, width = own.shape
    blocks, height, depth = database.shape
    parts = lax.axis_size("seq") * lax.axis_size("batch")
    slots = 2 * NBRS
    share = height // parts
    slab = lax.dynamic_slice_in_dim(database, lax.axis_index(COLUMN) * share, share, axis=1)
    pieces = [piece.reshape(-1, share, depth) for piece in plane_gather(slab)]
    wanted = (shard_ids[..., 0] * blocks + block_ids).reshape(1, slots)
    wanted = lax.all_gather(wanted, COLUMN, axis=0, tiled=True).reshape(-1)
    shard = lax.axis_index("db")
    place = jnp.stack([shard % SIDE, shard // SIDE, lax.axis_index("batch")]).astype(jnp.int32)
    chosen = pick(place, wanted, pieces, parts, slots)
    rows = lax.all_to_all(chosen, COLUMN, split_axis=0, concat_axis=0, tiled=True)
    rows = rows.reshape(parts, slots * share, depth)
    last = ring(own[tokens - 1 :], "seq", 1)
    gain = enc_gain.reshape(1, -1)
    prior_out = attend(0, rows, gain, kv_weight, own, last)
    back = ring(prior_out[SPAN - 1 :], "seq", -1)
    own_out = attend(1, rows, gain, kv_weight, own, own[SPAN - 1 : SPAN])
    first = lax.axis_index("seq") == 0
    head = jnp.where(first, jnp.zeros_like(prior_out), prior_out)[: SPAN - 1]
    result = jnp.concatenate([head, own_out[SPAN - 1 :], own_out[: SPAN - 1], back])
    return result[None]


def solution(mesh):
    in_specs = (
        P(("db", "batch"), "seq", None),
        P("db", None, None),
        P(),
        P(),
        P(("db", "batch"), "seq", None, None),
        P(("db", "batch"), "seq", None),
    )
    out_specs = P(("db", "batch"), "seq", None)
    return jax.shard_map(body, mesh=mesh, in_specs=in_specs, out_specs=out_specs, check_vma=False)
```

```python
import jax
import jax.numpy as jnp
from jax import lax
from jax.experimental import pallas as pl
from jax.experimental.pallas import tpu as pltpu
from jax.sharding import PartitionSpec as P

HEADS = 16
SPAN = 64
NBRS = 2
EPS = 1e-06
COLUMN = ("seq", "batch")
PLANE = ("db", "batch")
SIDE = 4
TILE = 512


def ring(value, axis, steps):
    count = lax.axis_size(axis)
    return lax.ppermute(value, axis, [(i, (i + steps) % count) for i in range(count)])


def shifted(place, along_x, steps):
    y, x = divmod(place, SIDE)
    return y * SIDE + (x + steps) % SIDE if along_x else (y + steps) % SIDE * SIDE + x


def plane_shift(value, stage, steps):
    pairs = []
    for place in range(lax.axis_size("db")):
        for core in range(lax.axis_size("batch")):
            goal = shifted(place, (core + stage) % 2 == 0, steps)
            pairs.append((place * 2 + core, goal * 2 + core))
    return lax.ppermute(value, PLANE, pairs)


def plane_gather(slab, later):
    first = {steps: plane_shift(slab, 0, steps) for steps in (1, 3, 2)}
    first = jnp.stack([slab] + [first[steps] for steps in (1, 2, 3)])
    first, later = lax.optimization_barrier((first, later))
    second = {steps: plane_shift(first, 1, steps) for steps in (1, 3, 2)}
    return [first] + [second[steps] for steps in (1, 2, 3)], later


def pick_kernel(place_ref, wanted_ref, *refs):
    pieces, out_ref, held_ref, sems = refs[:-3], refs[-3], refs[-2], refs[-1]
    count, slots = out_ref.shape[:2]
    cores = 2
    blocks = pieces[0].shape[0] // SIDE
    x, y, core = place_ref[0], place_ref[1], place_ref[2]

    def one(goal, slot, code):
        shard, block = code // blocks, code % blocks
        back_x = (x - shard % SIDE + SIDE) % SIDE
        back_y = (y - shard // SIDE + SIDE) % SIDE
        inner = jnp.where(core == 0, back_x, back_y)
        outer = jnp.where(core == 0, back_y, back_x)
        where = inner * blocks + block
        value = pieces[0][where]
        for step in range(1, SIDE):
            value = jnp.where(outer == step, pieces[step][where], value)
        held_ref[goal, slot] = value

    def send(goal):
        return pltpu.make_async_copy(held_ref.at[goal], out_ref.at[goal], sems.at[goal])

    def step(goal, carry):
        before = lax.rem(goal + count - cores, count)
        for slot in range(NBRS):
            one(goal, slot, wanted_ref[before * slots + NBRS + slot])
            one(goal, NBRS + slot, wanted_ref[goal * slots + slot])
        send(goal).start()
        return carry

    lax.fori_loop(0, count, step, 0, unroll=4)
    for goal in range(count):
        send(goal).wait()


def pick(place, wanted, pieces, count, slots):
    vmem = pl.BlockSpec(memory_space=pltpu.VMEM)
    smem = pl.BlockSpec(memory_space=pltpu.SMEM)
    shape = (count, slots) + pieces[0].shape[1:]
    return pl.pallas_call(
        pick_kernel,
        out_shape=pltpu.HBM(shape, pieces[0].dtype),
        in_specs=[smem, smem] + [vmem] * len(pieces),
        out_specs=pl.BlockSpec(memory_space=pltpu.HBM),
        scratch_shapes=[pltpu.VMEM(shape, pieces[0].dtype), pltpu.SemaphoreType.DMA((count,))],
        compiler_params=pltpu.CompilerParams(vmem_limit_bytes=8 * 2**20),
        name="pick",
    )(place, wanted, *pieces)


def prior_kernel(*refs):
    rows_ref, gain_ref, weight_ref, query_ref, spare_ref, out_ref, held_ref = refs[:7]
    sems = refs[-1]
    count = held_ref.shape[0]

    def load(piece):
        which, tile = divmod(piece, count // 2)
        columns = pl.ds(tile * TILE, TILE)
        return pltpu.make_async_copy(
            weight_ref.at[which, :, columns], held_ref.at[piece], sems.at[piece]
        )

    for piece in range(count):
        load(piece).start()
    attend_kernel(
        rows_ref, gain_ref, held_ref, query_ref, spare_ref, out_ref, *refs[7:-1], load=load
    )


def attend_kernel(
    rows_ref, gain_ref, held_ref, query_ref, spare_ref, out_ref,
    normed_ref, keys_ref, values_ref, score_ref, share_ref, load=None,
):
    width = query_ref.shape[1]
    head = width // HEADS
    tiles = width // TILE
    raw = rows_ref[...].reshape(normed_ref.shape).astype(jnp.float32)
    factor = lax.rsqrt(jnp.mean(raw * raw, axis=-1, keepdims=True) + EPS)
    normed_ref[...] = (raw * factor * gain_ref[...]).astype(jnp.bfloat16)

    def project(which, ref):
        for tile in range(tiles):
            if load is not None:
                load(which * tiles + tile).wait()
            product = jnp.dot(
                normed_ref[...], held_ref[which * tiles + tile], preferred_element_type=jnp.float32
            )
            ref[:, tile * TILE : (tile + 1) * TILE] = product.astype(jnp.bfloat16)

    project(0, keys_ref)
    bottom = lax.broadcasted_iota(jnp.int32, (SPAN, head), 0) == SPAN - 1
    heads = [
        (slice(h * head, (h + 1) * head), slice(h * SPAN, (h + 1) * SPAN)) for h in range(HEADS)
    ]
    for columns, place in heads:
        queries = jnp.where(
            bottom,
            spare_ref[:, columns].astype(jnp.float32),
            query_ref[:, columns].astype(jnp.float32),
        ).astype(jnp.bfloat16)
        scores = lax.dot_general(
            queries, keys_ref[:, columns], (((1,), (1,)), ((), ())), preferred_element_type=jnp.float32
        )
        score_ref[place] = scores * head ** (-0.5)
    for columns, place in heads:
        scores = score_ref[place]
        raised = jnp.exp(scores - jnp.max(scores, axis=-1, keepdims=True))
        total = jnp.sum(raised, axis=-1, keepdims=True)
        share_ref[place] = (raised * (1.0 / total)).astype(jnp.bfloat16)
    project(1, values_ref)
    for columns, place in heads:
        mixed = jnp.dot(share_ref[place], values_ref[:, columns], preferred_element_type=jnp.float32)
        out_ref[:, columns] = mixed.astype(out_ref.dtype)


def attend(span, rows, gain, weight, queries, spare):
    parts, height, depth = rows.shape
    tokens, width = queries.shape
    keys = parts * height // 2
    whole = pl.BlockSpec(memory_space=pltpu.VMEM)
    pieces = 2 * width // TILE
    out_shape = [jax.ShapeDtypeStruct((SPAN, width), queries.dtype)]
    out_specs = [pl.BlockSpec((SPAN, width), lambda i: (0, 0))]
    scratch_shapes = [
        pltpu.VMEM((keys, depth), jnp.bfloat16),
        pltpu.VMEM((keys, width), jnp.bfloat16),
        pltpu.VMEM((keys, width), jnp.bfloat16),
        pltpu.VMEM((HEADS * SPAN, keys), jnp.float32),
        pltpu.VMEM((HEADS * SPAN, keys), jnp.bfloat16),
    ]
    if span == 0:
        weight = pltpu.with_memory_space_constraint(weight, pltpu.HBM)
        out_shape.append(pltpu.VMEM((pieces, depth, TILE), weight.dtype))
        out_specs.append(whole)
        scratch_shapes.append(pltpu.SemaphoreType.DMA((pieces,)))
    flops = 4 * keys * depth * width
    return pl.pallas_call(
        prior_kernel if span == 0 else attend_kernel,
        grid=(1,),
        out_shape=out_shape,
        in_specs=[
            pl.BlockSpec((parts, height // 2, depth), lambda i: (0, span, 0)),
            whole,
            pl.BlockSpec(memory_space=pltpu.HBM) if span == 0 else whole,
            pl.BlockSpec((SPAN, width), lambda i: (span, 0)),
            whole,
        ],
        out_specs=out_specs,
        scratch_shapes=scratch_shapes,
        compiler_params=pltpu.CompilerParams(vmem_limit_bytes=20 * 2**20),
        cost_estimate=pl.CostEstimate(flops=flops, bytes_accessed=2**20, transcendentals=2**18),
        name="attend",
    )(rows, gain, weight, queries, spare)


def body(queries, database, enc_gain, kv_weight, shard_ids, block_ids):
    own = queries[0]
    tokens, width = own.shape
    blocks, height, depth = database.shape
    parts = lax.axis_size("seq") * lax.axis_size("batch")
    slots = 2 * NBRS
    share = height // parts
    slab = lax.dynamic_slice_in_dim(database, lax.axis_index(COLUMN) * share, share, axis=1)
    wanted = (shard_ids[..., 0] * blocks + block_ids).reshape(1, slots)
    wanted = jnp.broadcast_to(wanted, (parts, slots))
    pieces, wanted = plane_gather(slab, wanted)
    pieces = [piece.reshape(-1, share, depth) for piece in pieces]
    wanted = lax.all_to_all(wanted, COLUMN, split_axis=0, concat_axis=0, tiled=True).reshape(-1)
    shard = lax.axis_index("db")
    place = jnp.stack([shard % SIDE, shard // SIDE, lax.axis_index("batch")]).astype(jnp.int32)
    chosen = pick(place, wanted, pieces, parts, slots)
    rows = lax.all_to_all(chosen, COLUMN, split_axis=0, concat_axis=0, tiled=True)
    rows = rows.reshape(parts, slots * share, depth)
    last = ring(own[tokens - 1 :], "seq", 1)
    gain = enc_gain.reshape(1, -1)
    prior_out, held = attend(0, rows, gain, kv_weight, own, last)
    back = ring(prior_out[SPAN - 1 :], "seq", -1)
    [own_out] = attend(1, rows, gain, held, own, own[SPAN - 1 : SPAN])
    first = lax.axis_index("seq") == 0
    head = jnp.where(first, jnp.zeros_like(prior_out), prior_out)[: SPAN - 1]
    result = jnp.concatenate([head, own_out[SPAN - 1 :], own_out[: SPAN - 1], back])
    return result[None]


def solution(mesh):
    in_specs = (
        P(("db", "batch"), "seq", None),
        P("db", None, None),
        P(),
        P(),
        P(("db", "batch"), "seq", None, None),
        P(("db", "batch"), "seq", None),
    )
    out_specs = P(("db", "batch"), "seq", None)
    return jax.shard_map(body, mesh=mesh, in_specs=in_specs, out_specs=out_specs, check_vma=False)
```

```python
import jax
import jax.numpy as jnp
from jax import lax
from jax.experimental import pallas as pl
from jax.experimental.pallas import tpu as pltpu
from jax.sharding import PartitionSpec as P

HEADS = 16
SPAN = 64
NBRS = 2
EPS = 1e-06
COLUMN = ("seq", "batch")
PLANE = ("db", "batch")
SIDE = 4
TILE = 512


def ring(value, axis, steps):
    count = lax.axis_size(axis)
    return lax.ppermute(value, axis, [(i, (i + steps) % count) for i in range(count)])


def shifted(place, along_x, steps):
    y, x = divmod(place, SIDE)
    return y * SIDE + (x + steps) % SIDE if along_x else (y + steps) % SIDE * SIDE + x


def plane_shift(value, stage, steps):
    pairs = []
    for place in range(lax.axis_size("db")):
        for core in range(lax.axis_size("batch")):
            goal = shifted(place, (core + stage) % 2 == 0, steps)
            pairs.append((place * 2 + core, goal * 2 + core))
    return lax.ppermute(value, PLANE, pairs)


def plane_gather(slab, later):
    first = {steps: plane_shift(slab, 0, steps) for steps in (1, 3, 2)}
    first = jnp.stack([slab] + [first[steps] for steps in (1, 2, 3)])
    first, later = lax.optimization_barrier((first, later))
    second = {steps: plane_shift(first, 1, steps) for steps in (1, 3, 2)}
    return [first] + [second[steps] for steps in (1, 2, 3)], later


def front_kernel(place_ref, gain_ref, database_ref, out_ref, raw_ref, sem):
    height = raw_ref.shape[1]
    start = pl.multiple_of(place_ref[3] * height, height)
    copy = pltpu.make_async_copy(database_ref.at[:, pl.ds(start, height)], raw_ref, sem)
    copy.start()
    copy.wait()
    raw = raw_ref[...].astype(jnp.float32)
    own = jnp.where(place_ref[2] == 0, raw[:, : height // 2], raw[:, height // 2 :])
    factor = lax.rsqrt(jnp.mean(own * own, axis=-1, keepdims=True) + EPS)
    out_ref[...] = (own * factor * gain_ref[...]).astype(jnp.bfloat16)


def front(place, gain, database, share):
    blocks, _, depth = database.shape
    vmem = pl.BlockSpec(memory_space=pltpu.VMEM)
    return pl.pallas_call(
        front_kernel,
        out_shape=jax.ShapeDtypeStruct((blocks, share, depth), database.dtype),
        in_specs=[
            pl.BlockSpec(memory_space=pltpu.SMEM),
            vmem,
            pl.BlockSpec(memory_space=pltpu.HBM),
        ],
        out_specs=vmem,
        scratch_shapes=[
            pltpu.VMEM((blocks, 2 * share, depth), database.dtype),
            pltpu.SemaphoreType.DMA,
        ],
        compiler_params=pltpu.CompilerParams(vmem_limit_bytes=4 * 2**20),
        name="front",
    )(place, gain, pltpu.with_memory_space_constraint(database, pltpu.HBM))


def pick_kernel(place_ref, wanted_ref, *refs):
    pieces, out_ref, held_ref, sems = refs[:-3], refs[-3], refs[-2], refs[-1]
    count, slots = out_ref.shape[:2]
    blocks = pieces[0].shape[0] // SIDE
    x, y, core = place_ref[0], place_ref[1], place_ref[2]

    def one(goal, slot, code):
        shard, block = code // blocks, code % blocks
        back_x = (x - shard % SIDE + SIDE) % SIDE
        back_y = (y - shard // SIDE + SIDE) % SIDE
        inner = jnp.where(core == 0, back_x, back_y)
        outer = jnp.where(core == 0, back_y, back_x)
        where = inner * blocks + block
        value = pieces[0][where]
        for step in range(1, SIDE):
            value = jnp.where(outer == step, pieces[step][where], value)
        held_ref[goal, slot] = value

    def send(goal):
        return pltpu.make_async_copy(held_ref.at[goal], out_ref.at[goal], sems.at[goal])

    def step(goal, carry):
        before = lax.rem(goal + count - 2, count)
        for slot in range(NBRS):
            one(goal, slot, wanted_ref[before * slots + NBRS + slot])
            one(goal, NBRS + slot, wanted_ref[goal * slots + slot])
        send(goal).start()
        return carry

    lax.fori_loop(0, count, step, 0, unroll=4)
    for goal in range(count):
        send(goal).wait()


def pick(place, wanted, pieces, count, slots):
    smem = pl.BlockSpec(memory_space=pltpu.SMEM)
    shape = (count, slots) + pieces[0].shape[1:]
    return pl.pallas_call(
        pick_kernel,
        out_shape=pltpu.HBM(shape, pieces[0].dtype),
        in_specs=[smem, smem] + [pl.BlockSpec(memory_space=pltpu.VMEM)] * len(pieces),
        out_specs=pl.BlockSpec(memory_space=pltpu.HBM),
        scratch_shapes=[pltpu.VMEM(shape, pieces[0].dtype), pltpu.SemaphoreType.DMA((count,))],
        compiler_params=pltpu.CompilerParams(vmem_limit_bytes=8 * 2**20),
        name="pick",
    )(place, wanted, *pieces)


def prior_kernel(*refs):
    rows_ref, weight_ref, query_ref, spare_ref, out_ref, held_ref = refs[:6]
    sems = refs[-1]
    count = held_ref.shape[0]

    def load(piece):
        which, tile = divmod(piece, count // 2)
        columns = pl.ds(tile * TILE, TILE)
        return pltpu.make_async_copy(
            weight_ref.at[which, :, columns], held_ref.at[piece], sems.at[piece]
        )

    for piece in range(count):
        load(piece).start()
    attend_kernel(
        rows_ref, held_ref, query_ref, spare_ref, out_ref, *refs[6:-1], load=load
    )


def attend_kernel(
    rows_ref, held_ref, query_ref, spare_ref, out_ref,
    normed_ref, keys_ref, values_ref, score_ref, share_ref, load=None,
):
    width = query_ref.shape[1]
    head = width // HEADS
    tiles = width // TILE
    normed_ref[...] = rows_ref[...].reshape(normed_ref.shape)

    def project(which, ref):
        for tile in range(tiles):
            if load is not None:
                load(which * tiles + tile).wait()
            product = jnp.dot(
                normed_ref[...], held_ref[which * tiles + tile], preferred_element_type=jnp.float32
            )
            ref[:, tile * TILE : (tile + 1) * TILE] = product.astype(jnp.bfloat16)

    project(0, keys_ref)
    bottom = lax.broadcasted_iota(jnp.int32, (SPAN, head), 0) == SPAN - 1
    heads = [
        (slice(h * head, (h + 1) * head), slice(h * SPAN, (h + 1) * SPAN)) for h in range(HEADS)
    ]
    for columns, place in heads:
        queries = jnp.where(
            bottom,
            spare_ref[:, columns].astype(jnp.float32),
            query_ref[:, columns].astype(jnp.float32),
        ).astype(jnp.bfloat16)
        scores = lax.dot_general(
            queries, keys_ref[:, columns], (((1,), (1,)), ((), ())), preferred_element_type=jnp.float32
        )
        score_ref[place] = scores * head ** (-0.5)
    for columns, place in heads:
        scores = score_ref[place]
        raised = jnp.exp(scores - jnp.max(scores, axis=-1, keepdims=True))
        total = jnp.sum(raised, axis=-1, keepdims=True)
        share_ref[place] = (raised * (1.0 / total)).astype(jnp.bfloat16)
    project(1, values_ref)
    for columns, place in heads:
        mixed = jnp.dot(share_ref[place], values_ref[:, columns], preferred_element_type=jnp.float32)
        out_ref[:, columns] = mixed.astype(out_ref.dtype)


def attend(span, rows, weight, queries, spare):
    parts, height, depth = rows.shape
    tokens, width = queries.shape
    keys = parts * height // 2
    whole = pl.BlockSpec(memory_space=pltpu.VMEM)
    pieces = 2 * width // TILE
    out_shape = [jax.ShapeDtypeStruct((SPAN, width), queries.dtype)]
    out_specs = [pl.BlockSpec((SPAN, width), lambda i: (0, 0))]
    scratch_shapes = [
        pltpu.VMEM((keys, depth), jnp.bfloat16),
        pltpu.VMEM((keys, width), jnp.bfloat16),
        pltpu.VMEM((keys, width), jnp.bfloat16),
        pltpu.VMEM((HEADS * SPAN, keys), jnp.float32),
        pltpu.VMEM((HEADS * SPAN, keys), jnp.bfloat16),
    ]
    if span == 0:
        weight = pltpu.with_memory_space_constraint(weight, pltpu.HBM)
        out_shape.append(pltpu.VMEM((pieces, depth, TILE), weight.dtype))
        out_specs.append(whole)
        scratch_shapes.append(pltpu.SemaphoreType.DMA((pieces,)))
    flops = 4 * keys * depth * width
    return pl.pallas_call(
        prior_kernel if span == 0 else attend_kernel,
        grid=(1,),
        out_shape=out_shape,
        in_specs=[
            pl.BlockSpec((parts, height // 2, depth), lambda i: (0, span, 0)),
            pl.BlockSpec(memory_space=pltpu.HBM) if span == 0 else whole,
            pl.BlockSpec((SPAN, width), lambda i: (span, 0)),
            whole,
        ],
        out_specs=out_specs,
        scratch_shapes=scratch_shapes,
        compiler_params=pltpu.CompilerParams(vmem_limit_bytes=20 * 2**20),
        cost_estimate=pl.CostEstimate(flops=flops, bytes_accessed=2**20, transcendentals=2**18),
        name="attend",
    )(rows, weight, queries, spare)


def body(queries, database, enc_gain, kv_weight, shard_ids, block_ids):
    own = queries[0]
    tokens, width = own.shape
    blocks, height, depth = database.shape
    parts = lax.axis_size("seq") * lax.axis_size("batch")
    slots = 2 * NBRS
    share = height // parts
    shard = lax.axis_index("db")
    place = [shard % SIDE, shard // SIDE, lax.axis_index("batch"), lax.axis_index("seq")]
    place = jnp.stack(place).astype(jnp.int32)
    slab = front(place, enc_gain, database, share)
    wanted = (shard_ids[..., 0] * blocks + block_ids).reshape(1, slots)
    wanted = jnp.broadcast_to(wanted, (parts, slots))
    pieces, wanted = plane_gather(slab, wanted)
    wanted = lax.all_to_all(wanted, COLUMN, split_axis=0, concat_axis=0, tiled=True).reshape(-1)
    pieces = [piece.reshape(-1, share, depth) for piece in pieces]
    chosen = pick(place, wanted, pieces, parts, slots)
    rows = lax.all_to_all(chosen, COLUMN, split_axis=0, concat_axis=0, tiled=True)
    rows = rows.reshape(parts, slots * share, depth)
    last = ring(own[tokens - 1 :], "seq", 1)
    prior_out, held = attend(0, rows, kv_weight, own, last)
    back = ring(prior_out[SPAN - 1 :], "seq", -1)
    [own_out] = attend(1, rows, held, own, own[SPAN - 1 : SPAN])
    first = lax.axis_index("seq") == 0
    head = jnp.where(first, jnp.zeros_like(prior_out), prior_out)[: SPAN - 1]
    result = jnp.concatenate([head, own_out[SPAN - 1 :], own_out[: SPAN - 1], back])
    return result[None]


def solution(mesh):
    in_specs = (
        P(("db", "batch"), "seq", None),
        P("db", None, None),
        P(),
        P(),
        P(("db", "batch"), "seq", None, None),
        P(("db", "batch"), "seq", None),
    )
    out_specs = P(("db", "batch"), "seq", None)
    return jax.shard_map(body, mesh=mesh, in_specs=in_specs, out_specs=out_specs, check_vma=False)
```

```python
import jax
import jax.numpy as jnp
from jax import lax
from jax.experimental import pallas as pl
from jax.experimental.pallas import tpu as pltpu
from jax.sharding import PartitionSpec as P

HEADS = 16
SPAN = 64
NBRS = 2
EPS = 1e-06
COLUMN = ("seq", "batch")
PLANE = ("db", "batch")
SIDE = 4
TILE = 512


def ring(value, axis, steps):
    count = lax.axis_size(axis)
    return lax.ppermute(value, axis, [(i, (i + steps) % count) for i in range(count)])


def shifted(place, along_x, steps):
    y, x = divmod(place, SIDE)
    return y * SIDE + (x + steps) % SIDE if along_x else (y + steps) % SIDE * SIDE + x


def plane_shift(value, stage, steps):
    pairs = []
    for place in range(lax.axis_size("db")):
        for core in range(lax.axis_size("batch")):
            goal = shifted(place, (core + stage) % 2 == 0, steps)
            pairs.append((place * 2 + core, goal * 2 + core))
    return lax.ppermute(value, PLANE, pairs)


def plane_gather(slab, later):
    first = {steps: plane_shift(slab, 0, steps) for steps in (1, 3, 2)}
    first = jnp.stack([slab] + [first[steps] for steps in (1, 2, 3)])
    first, later = lax.optimization_barrier((first, later))
    second = {steps: plane_shift(first, 1, steps) for steps in (1, 3, 2)}
    return [first] + [second[steps] for steps in (1, 2, 3)], later


def front_kernel(place_ref, gain_hbm_ref, database_ref, out_ref, raw_ref, gain_ref, sem, gain_sem):
    gain = pltpu.make_async_copy(gain_hbm_ref, gain_ref, gain_sem)
    gain.start()
    height = raw_ref.shape[1]
    start = pl.multiple_of(place_ref[3] * height, height)
    copy = pltpu.make_async_copy(database_ref.at[:, pl.ds(start, height)], raw_ref, sem)
    copy.start()
    gain.wait()
    copy.wait()
    raw = raw_ref[...].astype(jnp.float32)
    own = jnp.where(place_ref[2] == 0, raw[:, : height // 2], raw[:, height // 2 :])
    factor = lax.rsqrt(jnp.mean(own * own, axis=-1, keepdims=True) + EPS)
    out_ref[...] = (own * factor * gain_ref[...]).astype(jnp.bfloat16)


def front(place, gain, database, share):
    blocks, _, depth = database.shape
    hbm = pl.BlockSpec(memory_space=pltpu.HBM)
    gain, database = (pltpu.with_memory_space_constraint(a, pltpu.HBM) for a in (gain, database))
    return pl.pallas_call(
        front_kernel,
        out_shape=jax.ShapeDtypeStruct((blocks, share, depth), database.dtype),
        in_specs=[
            pl.BlockSpec(memory_space=pltpu.SMEM),
            hbm,
            hbm,
        ],
        out_specs=pl.BlockSpec(memory_space=pltpu.VMEM),
        scratch_shapes=[
            pltpu.VMEM((blocks, 2 * share, depth), database.dtype),
            pltpu.VMEM(gain.shape, gain.dtype),
            pltpu.SemaphoreType.DMA,
            pltpu.SemaphoreType.DMA,
        ],
        compiler_params=pltpu.CompilerParams(vmem_limit_bytes=4 * 2**20),
        name="front",
    )(place, gain, database)


def pick_kernel(place_ref, wanted_ref, *refs):
    pieces, out_ref, held_ref, sems = refs[:-3], refs[-3], refs[-2], refs[-1]
    count, slots = out_ref.shape[:2]
    blocks = pieces[0].shape[0] // SIDE
    x, y, core = place_ref[0], place_ref[1], place_ref[2]

    def one(goal, slot, code):
        shard, block = code // blocks, code % blocks
        back_x = (x - shard % SIDE + SIDE) % SIDE
        back_y = (y - shard // SIDE + SIDE) % SIDE
        inner = jnp.where(core == 0, back_x, back_y)
        outer = jnp.where(core == 0, back_y, back_x)
        where = inner * blocks + block
        value = pieces[0][where]
        for step in range(1, SIDE):
            value = jnp.where(outer == step, pieces[step][where], value)
        held_ref[goal, slot] = value

    def send(goal):
        return pltpu.make_async_copy(held_ref.at[goal], out_ref.at[goal], sems.at[goal])

    def step(goal, carry):
        before = lax.rem(goal + count - 2, count)
        for slot in range(NBRS):
            one(goal, slot, wanted_ref[before * slots + NBRS + slot])
            one(goal, NBRS + slot, wanted_ref[goal * slots + slot])
        send(goal).start()
        return carry

    lax.fori_loop(0, count, step, 0, unroll=4)
    for goal in range(count):
        send(goal).wait()


def pick(place, wanted, pieces, count, slots):
    smem = pl.BlockSpec(memory_space=pltpu.SMEM)
    shape = (count, slots) + pieces[0].shape[1:]
    return pl.pallas_call(
        pick_kernel,
        out_shape=pltpu.HBM(shape, pieces[0].dtype),
        in_specs=[smem, smem] + [pl.BlockSpec(memory_space=pltpu.VMEM)] * len(pieces),
        out_specs=pl.BlockSpec(memory_space=pltpu.HBM),
        scratch_shapes=[pltpu.VMEM(shape, pieces[0].dtype), pltpu.SemaphoreType.DMA((count,))],
        compiler_params=pltpu.CompilerParams(vmem_limit_bytes=8 * 2**20),
        name="pick",
    )(place, wanted, *pieces)


def bring_kernel(source_ref, out_ref, sem):
    copy = pltpu.make_async_copy(source_ref.at[0, :, pl.ds(0, out_ref.shape[1])], out_ref, sem)
    copy.start()
    copy.wait()


def bring(weight, columns):
    return pl.pallas_call(
        bring_kernel,
        out_shape=pltpu.VMEM((weight.shape[1], columns), weight.dtype),
        in_specs=[pl.BlockSpec(memory_space=pltpu.HBM)],
        out_specs=pl.BlockSpec(memory_space=pltpu.VMEM),
        scratch_shapes=[pltpu.SemaphoreType.DMA],
        compiler_params=pltpu.CompilerParams(vmem_limit_bytes=2**22),
        name="bring",
    )(pltpu.with_memory_space_constraint(weight, pltpu.HBM))


def prior_kernel(*refs):
    rows_ref, tile_ref, weight_ref, query_ref, spare_ref, out_ref, held_ref = refs[:7]
    sems = refs[-1]
    tiles = weight_ref.shape[2] // TILE
    early = tile_ref.shape[1] // TILE

    def load(piece):
        which, tile = divmod(piece, tiles)
        columns = pl.ds(tile * TILE, TILE)
        return pltpu.make_async_copy(
            weight_ref.at[which, :, columns], held_ref.at[piece - early], sems.at[piece - early]
        )

    for piece in range(early, 2 * tiles):
        load(piece).start()
    attend_kernel(
        rows_ref, tile_ref, held_ref, query_ref, spare_ref, out_ref, *refs[7:-1], load=load
    )


def attend_kernel(
    rows_ref, tile_ref, held_ref, query_ref, spare_ref, out_ref,
    normed_ref, keys_ref, values_ref, score_ref, share_ref, load=None,
):
    width = query_ref.shape[1]
    head = width // HEADS
    tiles = width // TILE
    early = tile_ref.shape[1] // TILE
    normed_ref[...] = rows_ref[...].reshape(normed_ref.shape)

    def project(which, ref):
        for tile in range(tiles):
            columns = slice(tile * TILE, (tile + 1) * TILE)
            piece = which * tiles + tile
            if piece < early:
                weight = tile_ref[:, columns]
            else:
                if load is not None:
                    load(piece).wait()
                weight = held_ref[piece - early]
            product = jnp.dot(normed_ref[...], weight, preferred_element_type=jnp.float32)
            ref[:, columns] = product.astype(jnp.bfloat16)

    project(0, keys_ref)
    bottom = lax.broadcasted_iota(jnp.int32, (SPAN, head), 0) == SPAN - 1
    heads = [
        (slice(h * head, (h + 1) * head), slice(h * SPAN, (h + 1) * SPAN)) for h in range(HEADS)
    ]
    for columns, place in heads:
        queries = jnp.where(
            bottom,
            spare_ref[:, columns].astype(jnp.float32),
            query_ref[:, columns].astype(jnp.float32),
        ).astype(jnp.bfloat16)
        scores = lax.dot_general(
            queries, keys_ref[:, columns], (((1,), (1,)), ((), ())), preferred_element_type=jnp.float32
        )
        score_ref[place] = scores * head ** (-0.5)
    for columns, place in heads:
        scores = score_ref[place]
        raised = jnp.exp(scores - jnp.max(scores, axis=-1, keepdims=True))
        total = jnp.sum(raised, axis=-1, keepdims=True)
        share_ref[place] = (raised * (1.0 / total)).astype(jnp.bfloat16)
    project(1, values_ref)
    for columns, place in heads:
        mixed = jnp.dot(share_ref[place], values_ref[:, columns], preferred_element_type=jnp.float32)
        out_ref[:, columns] = mixed.astype(out_ref.dtype)


def attend(span, rows, weights, queries, spare):
    parts, height, depth = rows.shape
    tokens, width = queries.shape
    keys = parts * height // 2
    whole = pl.BlockSpec(memory_space=pltpu.VMEM)
    pieces = 2 * width // TILE - weights[0].shape[1] // TILE
    out_shape = [jax.ShapeDtypeStruct((SPAN, width), queries.dtype)]
    out_specs = [pl.BlockSpec((SPAN, width), lambda i: (0, 0))]
    scratch_shapes = [
        pltpu.VMEM((keys, depth), jnp.bfloat16),
        pltpu.VMEM((keys, width), jnp.bfloat16),
        pltpu.VMEM((keys, width), jnp.bfloat16),
        pltpu.VMEM((HEADS * SPAN, keys), jnp.float32),
        pltpu.VMEM((HEADS * SPAN, keys), jnp.bfloat16),
    ]
    if span == 0:
        weights = [weights[0], pltpu.with_memory_space_constraint(weights[1], pltpu.HBM)]
        out_shape.append(pltpu.VMEM((pieces, depth, TILE), rows.dtype))
        out_specs.append(whole)
        scratch_shapes.append(pltpu.SemaphoreType.DMA((pieces,)))
    flops = 4 * keys * depth * width
    return pl.pallas_call(
        prior_kernel if span == 0 else attend_kernel,
        grid=(1,),
        out_shape=out_shape,
        in_specs=[
            pl.BlockSpec((parts, height // 2, depth), lambda i: (0, span, 0)),
            whole,
            pl.BlockSpec(memory_space=pltpu.HBM) if span == 0 else whole,
            pl.BlockSpec((SPAN, width), lambda i: (span, 0)),
            whole,
        ],
        out_specs=out_specs,
        scratch_shapes=scratch_shapes,
        compiler_params=pltpu.CompilerParams(vmem_limit_bytes=20 * 2**20),
        cost_estimate=pl.CostEstimate(flops=flops, bytes_accessed=2**20, transcendentals=2**18),
        name="attend",
    )(rows, *weights, queries, spare)


def body(queries, database, enc_gain, kv_weight, shard_ids, block_ids):
    own = queries[0]
    tokens, width = own.shape
    blocks, height, depth = database.shape
    parts = lax.axis_size("seq") * lax.axis_size("batch")
    slots = 2 * NBRS
    share = height // parts
    shard = lax.axis_index("db")
    place = [shard % SIDE, shard // SIDE, lax.axis_index("batch"), lax.axis_index("seq")]
    place = jnp.stack(place).astype(jnp.int32)
    slab = front(place, enc_gain, database, share)
    wanted = shard_ids[..., 0] * blocks + block_ids
    wanted = jnp.broadcast_to(wanted, (parts,) + wanted.shape[1:])
    pieces, wanted = plane_gather(slab, wanted)
    wanted = lax.all_to_all(wanted, COLUMN, split_axis=0, concat_axis=0, tiled=True).reshape(-1)
    pieces = [piece.reshape(-1, share, depth) for piece in pieces]
    chosen = pick(place, wanted, pieces, parts, slots)
    chosen, kv_weight = lax.optimization_barrier((chosen, kv_weight))
    tile = bring(kv_weight, 2 * TILE)
    rows = lax.all_to_all(chosen, COLUMN, split_axis=0, concat_axis=0, tiled=True)
    rows = rows.reshape(parts, slots * share, depth)
    last = ring(own[tokens - 1 :], "seq", 1)
    prior_out, held = attend(0, rows, [tile, kv_weight], own, last)
    back = ring(prior_out[SPAN - 1 :], "seq", -1)
    [own_out] = attend(1, rows, [tile, held], own, own[SPAN - 1 : SPAN])
    first = lax.axis_index("seq") == 0
    head = jnp.where(first, jnp.zeros_like(prior_out), prior_out)[: SPAN - 1]
    result = jnp.concatenate([head, own_out[SPAN - 1 :], own_out[: SPAN - 1], back])
    return result[None]


def solution(mesh):
    in_specs = (
        P(("db", "batch"), "seq", None),
        P("db", None, None),
        P(),
        P(),
        P(("db", "batch"), "seq", None, None),
        P(("db", "batch"), "seq", None),
    )
    out_specs = P(("db", "batch"), "seq", None)
    return jax.shard_map(body, mesh=mesh, in_specs=in_specs, out_specs=out_specs, check_vma=False)
```

```python
import jax
import jax.numpy as jnp
from jax import lax
from jax.experimental import pallas as pl
from jax.experimental.pallas import tpu as pltpu
from jax.sharding import PartitionSpec as P

HEADS = 16
SPAN = 64
NBRS = 2
EPS = 1e-06
COLUMN = ("seq", "batch")
PLANE = ("db", "batch")
SIDE = 4
TILE = 512


def ring(value, axis, steps):
    count = lax.axis_size(axis)
    return lax.ppermute(value, axis, [(i, (i + steps) % count) for i in range(count)])


def shifted(place, along_x, steps):
    y, x = divmod(place, SIDE)
    return y * SIDE + (x + steps) % SIDE if along_x else (y + steps) % SIDE * SIDE + x


def plane_shift(value, stage, steps):
    pairs = []
    for place in range(lax.axis_size("db")):
        for core in range(lax.axis_size("batch")):
            goal = shifted(place, (core + stage) % 2 == 0, steps)
            pairs.append((place * 2 + core, goal * 2 + core))
    return lax.ppermute(value, PLANE, pairs)


def plane_gather(slab, later):
    first = {steps: plane_shift(slab, 0, steps) for steps in (1, 3, 2)}
    first = jnp.stack([slab] + [first[steps] for steps in (1, 2, 3)])
    first, later = lax.optimization_barrier((first, later))
    second = {steps: plane_shift(first, 1, steps) for steps in (1, 3, 2)}
    return [first] + [second[steps] for steps in (1, 2, 3)], later


def front_kernel(place_ref, gain_hbm_ref, database_ref, out_ref, raw_ref, gain_ref, sem, gain_sem):
    gain = pltpu.make_async_copy(gain_hbm_ref, gain_ref, gain_sem)
    gain.start()
    height = raw_ref.shape[1]
    start = pl.multiple_of(place_ref[3] * height, height)
    copy = pltpu.make_async_copy(database_ref.at[:, pl.ds(start, height)], raw_ref, sem)
    copy.start()
    gain.wait()
    copy.wait()
    raw = raw_ref[...].astype(jnp.float32)
    own = jnp.where(place_ref[2] == 0, raw[:, : height // 2], raw[:, height // 2 :])
    factor = lax.rsqrt(jnp.mean(own * own, axis=-1, keepdims=True) + EPS)
    out_ref[...] = (own * factor * gain_ref[...]).astype(jnp.bfloat16)


def front(place, gain, database, share):
    blocks, _, depth = database.shape
    hbm = pl.BlockSpec(memory_space=pltpu.HBM)
    gain, database = (pltpu.with_memory_space_constraint(a, pltpu.HBM) for a in (gain, database))
    return pl.pallas_call(
        front_kernel,
        out_shape=jax.ShapeDtypeStruct((blocks, share, depth), database.dtype),
        in_specs=[
            pl.BlockSpec(memory_space=pltpu.SMEM),
            hbm,
            hbm,
        ],
        out_specs=pl.BlockSpec(memory_space=pltpu.VMEM),
        scratch_shapes=[
            pltpu.VMEM((blocks, 2 * share, depth), database.dtype),
            pltpu.VMEM(gain.shape, gain.dtype),
            pltpu.SemaphoreType.DMA,
            pltpu.SemaphoreType.DMA,
        ],
        compiler_params=pltpu.CompilerParams(vmem_limit_bytes=4 * 2**20),
        name="front",
    )(place, gain, database)


def pick_kernel(place_ref, wanted_ref, *refs):
    pieces, out_ref, held_ref, sems = refs[:-3], refs[-3], refs[-2], refs[-1]
    count, slots = out_ref.shape[:2]
    blocks = pieces[0].shape[0] // SIDE
    x, y, core = place_ref[0], place_ref[1], place_ref[2]

    def one(goal, slot, code):
        shard, block = code >> blocks.bit_length() - 1, code & blocks - 1
        back_x = x - (shard & SIDE - 1) & SIDE - 1
        back_y = y - (shard >> SIDE.bit_length() - 1) & SIDE - 1
        inner = jnp.where(core == 0, back_x, back_y)
        outer = jnp.where(core == 0, back_y, back_x)
        where = inner * blocks + block
        value = pieces[0][where]
        for step in range(1, SIDE):
            value = jnp.where(outer == step, pieces[step][where], value)
        held_ref[goal, slot] = value

    def send(goal):
        return pltpu.make_async_copy(held_ref.at[goal], out_ref.at[goal], sems.at[goal])

    def step(goal, carry):
        before = lax.rem(goal + count - 2, count)
        for slot in range(NBRS):
            one(goal, slot, wanted_ref[before * slots + NBRS + slot])
            one(goal, NBRS + slot, wanted_ref[goal * slots + slot])
        send(goal).start()
        return carry

    lax.fori_loop(0, count, step, 0, unroll=4)
    for goal in range(count):
        send(goal).wait()


def pick(place, wanted, pieces, count, slots):
    smem = pl.BlockSpec(memory_space=pltpu.SMEM)
    shape = (count, slots) + pieces[0].shape[1:]
    assert all(size & size - 1 == 0 for size in (SIDE, pieces[0].shape[0]))
    return pl.pallas_call(
        pick_kernel,
        out_shape=pltpu.HBM(shape, pieces[0].dtype),
        in_specs=[smem, smem] + [pl.BlockSpec(memory_space=pltpu.VMEM)] * len(pieces),
        out_specs=pl.BlockSpec(memory_space=pltpu.HBM),
        scratch_shapes=[pltpu.VMEM(shape, pieces[0].dtype), pltpu.SemaphoreType.DMA((count,))],
        compiler_params=pltpu.CompilerParams(vmem_limit_bytes=8 * 2**20),
        name="pick",
    )(place, wanted, *pieces)


def bring_kernel(source_ref, out_ref, sem):
    copy = pltpu.make_async_copy(source_ref.at[0, :, pl.ds(0, out_ref.shape[1])], out_ref, sem)
    copy.start()
    copy.wait()


def bring(weight, columns):
    return pl.pallas_call(
        bring_kernel,
        out_shape=pltpu.VMEM((weight.shape[1], columns), weight.dtype),
        in_specs=[pl.BlockSpec(memory_space=pltpu.HBM)],
        out_specs=pl.BlockSpec(memory_space=pltpu.VMEM),
        scratch_shapes=[pltpu.SemaphoreType.DMA],
        compiler_params=pltpu.CompilerParams(vmem_limit_bytes=2**22),
        name="bring",
    )(pltpu.with_memory_space_constraint(weight, pltpu.HBM))


def prior_kernel(*refs):
    rows_ref, tile_ref, weight_ref, query_ref, spare_ref, out_ref, held_ref = refs[:7]
    sems = refs[-1]
    tiles = weight_ref.shape[2] // TILE
    early = tile_ref.shape[1] // TILE

    def load(piece):
        which, tile = divmod(piece, tiles)
        columns = pl.ds(tile * TILE, TILE)
        return pltpu.make_async_copy(
            weight_ref.at[which, :, columns], held_ref.at[piece - early], sems.at[piece - early]
        )

    for piece in range(early, 2 * tiles):
        load(piece).start()
    attend_kernel(
        rows_ref, tile_ref, held_ref, query_ref, spare_ref, out_ref, *refs[7:-1], load=load
    )


def attend_kernel(
    rows_ref, tile_ref, held_ref, query_ref, spare_ref, out_ref,
    normed_ref, keys_ref, values_ref, score_ref, share_ref, load=None,
):
    width = query_ref.shape[1]
    head = width // HEADS
    tiles = width // TILE
    early = tile_ref.shape[1] // TILE
    normed_ref[...] = rows_ref[...].reshape(normed_ref.shape)

    def project(which, ref):
        for tile in range(tiles):
            columns = slice(tile * TILE, (tile + 1) * TILE)
            piece = which * tiles + tile
            if piece < early:
                weight = tile_ref[:, columns]
            else:
                if load is not None:
                    load(piece).wait()
                weight = held_ref[piece - early]
            product = jnp.dot(normed_ref[...], weight, preferred_element_type=jnp.float32)
            ref[:, columns] = product.astype(jnp.bfloat16)

    project(0, keys_ref)
    bottom = lax.broadcasted_iota(jnp.int32, (SPAN, head), 0) == SPAN - 1
    heads = [
        (slice(h * head, (h + 1) * head), slice(h * SPAN, (h + 1) * SPAN)) for h in range(HEADS)
    ]
    for columns, place in heads:
        queries = jnp.where(
            bottom,
            spare_ref[:, columns].astype(jnp.float32),
            query_ref[:, columns].astype(jnp.float32),
        ).astype(jnp.bfloat16)
        scores = lax.dot_general(
            queries, keys_ref[:, columns], (((1,), (1,)), ((), ())), preferred_element_type=jnp.float32
        )
        score_ref[place] = scores * head ** (-0.5)
    for columns, place in heads:
        scores = score_ref[place]
        raised = jnp.exp(scores - jnp.max(scores, axis=-1, keepdims=True))
        total = jnp.sum(raised, axis=-1, keepdims=True)
        share_ref[place] = (raised * (1.0 / total)).astype(jnp.bfloat16)
    project(1, values_ref)
    for columns, place in heads:
        mixed = jnp.dot(share_ref[place], values_ref[:, columns], preferred_element_type=jnp.float32)
        out_ref[:, columns] = mixed.astype(out_ref.dtype)


def attend(span, rows, weights, queries, spare):
    parts, height, depth = rows.shape
    tokens, width = queries.shape
    keys = parts * height // 2
    whole = pl.BlockSpec(memory_space=pltpu.VMEM)
    pieces = 2 * width // TILE - weights[0].shape[1] // TILE
    out_shape = [jax.ShapeDtypeStruct((SPAN, width), queries.dtype)]
    out_specs = [pl.BlockSpec((SPAN, width), lambda i: (0, 0))]
    scratch_shapes = [
        pltpu.VMEM((keys, depth), jnp.bfloat16),
        pltpu.VMEM((keys, width), jnp.bfloat16),
        pltpu.VMEM((keys, width), jnp.bfloat16),
        pltpu.VMEM((HEADS * SPAN, keys), jnp.float32),
        pltpu.VMEM((HEADS * SPAN, keys), jnp.bfloat16),
    ]
    if span == 0:
        weights = [weights[0], pltpu.with_memory_space_constraint(weights[1], pltpu.HBM)]
        out_shape.append(pltpu.VMEM((pieces, depth, TILE), rows.dtype))
        out_specs.append(whole)
        scratch_shapes.append(pltpu.SemaphoreType.DMA((pieces,)))
    flops = 4 * keys * depth * width
    return pl.pallas_call(
        prior_kernel if span == 0 else attend_kernel,
        grid=(1,),
        out_shape=out_shape,
        in_specs=[
            pl.BlockSpec((parts, height // 2, depth), lambda i: (0, span, 0)),
            whole,
            pl.BlockSpec(memory_space=pltpu.HBM) if span == 0 else whole,
            pl.BlockSpec((SPAN, width), lambda i: (span, 0)),
            whole,
        ],
        out_specs=out_specs,
        scratch_shapes=scratch_shapes,
        compiler_params=pltpu.CompilerParams(vmem_limit_bytes=20 * 2**20),
        cost_estimate=pl.CostEstimate(flops=flops, bytes_accessed=2**20, transcendentals=2**18),
        name="attend",
    )(rows, *weights, queries, spare)


def body(queries, database, enc_gain, kv_weight, shard_ids, block_ids):
    own = queries[0]
    tokens, width = own.shape
    blocks, height, depth = database.shape
    parts = lax.axis_size("seq") * lax.axis_size("batch")
    slots = 2 * NBRS
    share = height // parts
    shard = lax.axis_index("db")
    place = [shard % SIDE, shard // SIDE, lax.axis_index("batch"), lax.axis_index("seq")]
    place = jnp.stack(place).astype(jnp.int32)
    slab = front(place, enc_gain, database, share)
    wanted = shard_ids[..., 0] * blocks + block_ids
    wanted = jnp.broadcast_to(wanted, (parts,) + wanted.shape[1:])
    pieces, wanted = plane_gather(slab, wanted)
    wanted = lax.all_to_all(wanted, COLUMN, split_axis=0, concat_axis=0, tiled=True).reshape(-1)
    pieces = [piece.reshape(-1, share, depth) for piece in pieces]
    chosen = pick(place, wanted, pieces, parts, slots)
    chosen, kv_weight = lax.optimization_barrier((chosen, kv_weight))
    tile = bring(kv_weight, 2 * TILE)
    rows = lax.all_to_all(chosen, COLUMN, split_axis=0, concat_axis=0, tiled=True)
    rows = rows.reshape(parts, slots * share, depth)
    last = ring(own[tokens - 1 :], "seq", 1)
    prior_out, held = attend(0, rows, [tile, kv_weight], own, last)
    back = ring(prior_out[SPAN - 1 :], "seq", -1)
    [own_out] = attend(1, rows, [tile, held], own, own[SPAN - 1 : SPAN])
    first = lax.axis_index("seq") == 0
    head = jnp.where(first, jnp.zeros_like(prior_out), prior_out)[: SPAN - 1]
    result = jnp.concatenate([head, own_out[SPAN - 1 :], own_out[: SPAN - 1], back])
    return result[None]


def solution(mesh):
    in_specs = (
        P(("db", "batch"), "seq", None),
        P("db", None, None),
        P(),
        P(),
        P(("db", "batch"), "seq", None, None),
        P(("db", "batch"), "seq", None),
    )
    out_specs = P(("db", "batch"), "seq", None)
    return jax.shard_map(body, mesh=mesh, in_specs=in_specs, out_specs=out_specs, check_vma=False)
```

```python
import functools

import jax
import jax.numpy as jnp
from jax import lax
from jax.experimental import pallas as pl
from jax.experimental.pallas import tpu as pltpu
from jax.sharding import PartitionSpec as P

HEADS = 16
SPAN = 64
NBRS = 2
EPS = 1e-06
COLUMN = ("seq", "batch")
PLANE = ("db", "batch")
SIDE = 4
TILE = 512
NEAR = (1, 7, 2, 6)
FAR = (3, 5, 4)


def ring(value, axis, steps):
    count = lax.axis_size(axis)
    return lax.ppermute(value, axis, [(i, (i + steps) % count) for i in range(count)])


def shifted(place, along_x, steps):
    y, x = divmod(place, SIDE)
    return y * SIDE + (x + steps) % SIDE if along_x else (y + steps) % SIDE * SIDE + x


def plane_shift(value, stage, steps):
    pairs = []
    for place in range(lax.axis_size("db")):
        for core in range(lax.axis_size("batch")):
            goal = shifted(place, (core + stage) % 2 == 0, steps)
            pairs.append((place * 2 + core, goal * 2 + core))
    return lax.ppermute(value, PLANE, pairs)


def plane_gather(slab, later):
    first = {steps: plane_shift(slab, 0, steps) for steps in (1, 3, 2)}
    first = jnp.stack([slab] + [first[steps] for steps in (1, 2, 3)])
    first, later = lax.optimization_barrier((first, later))
    second = {steps: plane_shift(first, 1, steps) for steps in (1, 3, 2)}
    return [first] + [second[steps] for steps in (1, 2, 3)], later


def front_kernel(place_ref, gain_hbm_ref, database_ref, out_ref, raw_ref, gain_ref, sem, gain_sem):
    gain = pltpu.make_async_copy(gain_hbm_ref, gain_ref, gain_sem)
    gain.start()
    height = raw_ref.shape[1]
    start = pl.multiple_of(place_ref[3] * height, height)
    copy = pltpu.make_async_copy(database_ref.at[:, pl.ds(start, height)], raw_ref, sem)
    copy.start()
    gain.wait()
    copy.wait()
    raw = raw_ref[...].astype(jnp.float32)
    own = jnp.where(place_ref[2] == 0, raw[:, : height // 2], raw[:, height // 2 :])
    factor = lax.rsqrt(jnp.mean(own * own, axis=-1, keepdims=True) + EPS)
    out_ref[...] = (own * factor * gain_ref[...]).astype(jnp.bfloat16)


def front(place, gain, database, share):
    blocks, _, depth = database.shape
    hbm = pl.BlockSpec(memory_space=pltpu.HBM)
    gain, database = (pltpu.with_memory_space_constraint(a, pltpu.HBM) for a in (gain, database))
    return pl.pallas_call(
        front_kernel,
        out_shape=jax.ShapeDtypeStruct((blocks, share, depth), database.dtype),
        in_specs=[
            pl.BlockSpec(memory_space=pltpu.SMEM),
            hbm,
            hbm,
        ],
        out_specs=pl.BlockSpec(memory_space=pltpu.VMEM),
        scratch_shapes=[
            pltpu.VMEM((blocks, 2 * share, depth), database.dtype),
            pltpu.VMEM(gain.shape, gain.dtype),
            pltpu.SemaphoreType.DMA,
            pltpu.SemaphoreType.DMA,
        ],
        compiler_params=pltpu.CompilerParams(vmem_limit_bytes=4 * 2**20),
        name="front",
    )(place, gain, database)


def pick_kernel(place_ref, wanted_ref, *refs):
    pieces, outs, held_ref, sems = refs[:SIDE], refs[SIDE:-2], refs[-2], refs[-1]
    cores, slots = held_ref.shape[1:3]
    seq = len(outs)
    blocks = pieces[0].shape[0] // SIDE
    x, y, core, place = place_ref[0], place_ref[1], place_ref[2], place_ref[3]

    def one(code):
        shard, block = code >> blocks.bit_length() - 1, code & blocks - 1
        back_x = x - (shard & SIDE - 1) & SIDE - 1
        back_y = y - (shard >> SIDE.bit_length() - 1) & SIDE - 1
        inner = jnp.where(core == 0, back_x, back_y)
        outer = jnp.where(core == 0, back_y, back_x)
        where = inner * blocks + block
        value = pieces[0][where]
        for step in range(1, SIDE):
            value = jnp.where(outer == step, pieces[step][where], value)
        return value

    copies = [pltpu.make_async_copy(held_ref.at[k - 1], outs[k], sems.at[k - 1]) for k in range(1, seq)]
    for k in NEAR + FAR + (0,):
        goal_ref = held_ref.at[k - 1] if k else outs[0]
        for other in range(cores):
            side = core ^ other
            here = ((place + k & seq - 1) * cores + side) * slots
            before = ((place + k - 1 & seq - 1) * cores + side) * slots
            for slot in range(NBRS):
                goal_ref[other, slot] = one(wanted_ref[before + NBRS + slot])
                goal_ref[other, NBRS + slot] = one(wanted_ref[here + slot])
        if k:
            copies[k - 1].start()
    for copy in copies:
        copy.wait()


def pick(place, wanted, pieces, seq, cores, slots):
    smem = pl.BlockSpec(memory_space=pltpu.SMEM)
    shape = (cores, slots) + pieces[0].shape[1:]
    assert all(size & size - 1 == 0 for size in (SIDE, pieces[0].shape[0], seq, cores))
    return pl.pallas_call(
        pick_kernel,
        out_shape=[pltpu.VMEM(shape, pieces[0].dtype)]
        + [pltpu.HBM(shape, pieces[0].dtype)] * (seq - 1),
        in_specs=[smem, smem] + [pl.BlockSpec(memory_space=pltpu.VMEM)] * len(pieces),
        out_specs=[pl.BlockSpec(memory_space=pltpu.VMEM)]
        + [pl.BlockSpec(memory_space=pltpu.HBM)] * (seq - 1),
        scratch_shapes=[
            pltpu.VMEM((seq - 1,) + shape, pieces[0].dtype),
            pltpu.SemaphoreType.DMA((seq - 1,)),
        ],
        compiler_params=pltpu.CompilerParams(vmem_limit_bytes=8 * 2**20),
        name="pick",
    )(place, wanted, *pieces)


def pack_kernel(*refs):
    for part, ref in enumerate(refs[:-1]):
        refs[-1][part] = ref[1]


def pack(arrays):
    vmem = pl.BlockSpec(memory_space=pltpu.VMEM)
    return pl.pallas_call(
        pack_kernel,
        out_shape=jax.ShapeDtypeStruct((len(arrays),) + arrays[0].shape[1:], arrays[0].dtype),
        in_specs=[vmem] * len(arrays),
        out_specs=vmem,
        compiler_params=pltpu.CompilerParams(vmem_limit_bytes=4 * 2**20),
        name="pack",
    )(*arrays)


def column_rows(chosen, tile, behind):
    flat = lambda value: value.reshape(value.shape[0], -1, value.shape[-1])
    got = {k: ring(chosen[k], "seq", k) for k in NEAR}
    far = [chosen[k] for k in FAR]
    far, got[NEAR[0]] = lax.optimization_barrier((far, got[NEAR[0]]))
    got.update({k: ring(value, "seq", k) for k, value in zip(FAR, far)})
    behind, got[NEAR[3]] = lax.optimization_barrier((behind, got[NEAR[3]]))
    behind = ring(behind, "seq", 1)
    got[0] = chosen[0]
    order = (0,) + NEAR + FAR
    got, tile = lax.optimization_barrier((got, tile))
    other = lax.ppermute(pack([got[k] for k in order]), "batch", [(0, 1), (1, 0)])
    return [(flat(got[k]), 1) for k in order] + [(flat(other), len(order))], tile, behind


def bring_kernel(source_ref, out_ref, sem):
    copy = pltpu.make_async_copy(source_ref.at[0, :, pl.ds(0, out_ref.shape[1])], out_ref, sem)
    copy.start()
    copy.wait()


def bring(weight, columns):
    return pl.pallas_call(
        bring_kernel,
        out_shape=pltpu.VMEM((weight.shape[1], columns), weight.dtype),
        in_specs=[pl.BlockSpec(memory_space=pltpu.HBM)],
        out_specs=pl.BlockSpec(memory_space=pltpu.VMEM),
        scratch_shapes=[pltpu.SemaphoreType.DMA],
        compiler_params=pltpu.CompilerParams(vmem_limit_bytes=2**22),
        name="bring",
    )(pltpu.with_memory_space_constraint(weight, pltpu.HBM))


def prior_kernel(counts, *refs):
    tile_ref, weight_ref, query_ref, spare_ref, *rest = refs
    rows_refs, (out_ref, held_ref, *scratch, sems) = rest[:-8], rest[-8:]
    tiles = weight_ref.shape[2] // TILE
    early = tile_ref.shape[1] // TILE

    def load(piece):
        which, tile = divmod(piece, tiles)
        columns = pl.ds(tile * TILE, TILE)
        return pltpu.make_async_copy(
            weight_ref.at[which, :, columns], held_ref.at[piece - early], sems.at[piece - early]
        )

    for piece in range(early, 2 * tiles):
        load(piece).start()
    attend_kernel(
        counts, tile_ref, held_ref, query_ref, spare_ref, *rows_refs, out_ref, *scratch, span=0, load=load
    )


def attend_kernel(counts, *refs, span=1, load=None):
    tile_ref, held_ref, query_ref, spare_ref, *rest = refs
    rows_refs, rest = rest[:-6], rest[-6:]
    out_ref, normed_ref, keys_ref, values_ref, score_ref, share_ref = rest
    width = query_ref.shape[1]
    head = width // HEADS
    tiles = width // TILE
    early = tile_ref.shape[1] // TILE
    at = 0
    for rows_ref, parts in zip(rows_refs, counts):
        _, height, depth = rows_ref.shape
        share = height // 2
        size = parts * share
        rows = rows_ref[:parts, span * share : (span + 1) * share]
        normed_ref[at : at + size] = rows.reshape(size, depth)
        at += size

    def project(which, ref):
        for tile in range(tiles):
            columns = slice(tile * TILE, (tile + 1) * TILE)
            piece = which * tiles + tile
            if piece < early:
                weight = tile_ref[:, columns]
            else:
                if load is not None:
                    load(piece).wait()
                weight = held_ref[piece - early]
            product = jnp.dot(normed_ref[...], weight, preferred_element_type=jnp.float32)
            ref[:, columns] = product.astype(jnp.bfloat16)

    project(0, keys_ref)
    bottom = lax.broadcasted_iota(jnp.int32, (SPAN, head), 0) == SPAN - 1
    heads = [
        (slice(h * head, (h + 1) * head), slice(h * SPAN, (h + 1) * SPAN)) for h in range(HEADS)
    ]
    for columns, place in heads:
        queries = jnp.where(
            bottom,
            spare_ref[:, columns].astype(jnp.float32),
            query_ref[:, columns].astype(jnp.float32),
        ).astype(jnp.bfloat16)
        scores = lax.dot_general(
            queries, keys_ref[:, columns], (((1,), (1,)), ((), ())), preferred_element_type=jnp.float32
        )
        score_ref[place] = scores * head ** (-0.5)
    for columns, place in heads:
        scores = score_ref[place]
        raised = jnp.exp(scores - jnp.max(scores, axis=-1, keepdims=True))
        total = jnp.sum(raised, axis=-1, keepdims=True)
        share_ref[place] = (raised * (1.0 / total)).astype(jnp.bfloat16)
    project(1, values_ref)
    for columns, place in heads:
        mixed = jnp.dot(share_ref[place], values_ref[:, columns], preferred_element_type=jnp.float32)
        out_ref[:, columns] = mixed.astype(out_ref.dtype)


def attend(span, rows, weights, queries, spare):
    rows, counts = zip(*rows)
    _, height, depth = rows[0].shape
    tokens, width = queries.shape
    keys = sum(counts) * height // 2
    whole = pl.BlockSpec(memory_space=pltpu.VMEM)
    pieces = 2 * width // TILE - weights[0].shape[1] // TILE
    out_shape = [jax.ShapeDtypeStruct((SPAN, width), queries.dtype)]
    out_specs = [pl.BlockSpec((SPAN, width), lambda i: (0, 0))]
    scratch_shapes = [
        pltpu.VMEM((keys, depth), jnp.bfloat16),
        pltpu.VMEM((keys, width), jnp.bfloat16),
        pltpu.VMEM((keys, width), jnp.bfloat16),
        pltpu.VMEM((HEADS * SPAN, keys), jnp.float32),
        pltpu.VMEM((HEADS * SPAN, keys), jnp.bfloat16),
    ]
    if span == 0:
        weights = [weights[0], pltpu.with_memory_space_constraint(weights[1], pltpu.HBM)]
        out_shape.append(pltpu.VMEM((pieces, depth, TILE), queries.dtype))
        out_specs.append(whole)
        scratch_shapes.append(pltpu.SemaphoreType.DMA((pieces,)))
    flops = 4 * keys * depth * width
    return pl.pallas_call(
        functools.partial(prior_kernel if span == 0 else attend_kernel, counts),
        grid=(1,),
        out_shape=out_shape,
        in_specs=[
            whole,
            pl.BlockSpec(memory_space=pltpu.HBM) if span == 0 else whole,
            pl.BlockSpec((SPAN, width), lambda i: (span, 0)),
            whole,
            *[whole] * len(rows),
        ],
        out_specs=out_specs,
        scratch_shapes=scratch_shapes,
        compiler_params=pltpu.CompilerParams(vmem_limit_bytes=20 * 2**20),
        cost_estimate=pl.CostEstimate(flops=flops, bytes_accessed=2**20, transcendentals=2**18),
        name="attend",
    )(*weights, queries, spare, *rows)


def body(queries, database, enc_gain, kv_weight, shard_ids, block_ids):
    own = queries[0]
    tokens, width = own.shape
    blocks, height, depth = database.shape
    parts = lax.axis_size("seq") * lax.axis_size("batch")
    slots = 2 * NBRS
    share = height // parts
    shard = lax.axis_index("db")
    place = [shard % SIDE, shard // SIDE, lax.axis_index("batch"), lax.axis_index("seq")]
    place = jnp.stack(place).astype(jnp.int32)
    slab = front(place, enc_gain, database, share)
    wanted = shard_ids[..., 0] * blocks + block_ids
    wanted = jnp.broadcast_to(wanted, (parts,) + wanted.shape[1:])
    pieces, wanted = plane_gather(slab, wanted)
    wanted = lax.all_to_all(wanted, COLUMN, split_axis=0, concat_axis=0, tiled=True).reshape(-1)
    pieces = [piece.reshape(-1, share, depth) for piece in pieces]
    chosen = pick(place, wanted, pieces, lax.axis_size("seq"), lax.axis_size("batch"), slots)
    chosen, kv_weight = lax.optimization_barrier((chosen, kv_weight))
    tile = bring(kv_weight, TILE)
    rows, tile, last = column_rows(chosen, tile, own[tokens - 1 :])
    prior_out, held = attend(0, rows, [tile, kv_weight], own, last)
    back = ring(prior_out[SPAN - 1 :], "seq", -1)
    [own_out] = attend(1, rows, [tile, held], own, own[SPAN - 1 : SPAN])
    first = lax.axis_index("seq") == 0
    head = jnp.where(first, jnp.zeros_like(prior_out), prior_out)[: SPAN - 1]
    result = jnp.concatenate([head, own_out[SPAN - 1 :], own_out[: SPAN - 1], back])
    return result[None]


def solution(mesh):
    in_specs = (
        P(("db", "batch"), "seq", None),
        P("db", None, None),
        P(),
        P(),
        P(("db", "batch"), "seq", None, None),
        P(("db", "batch"), "seq", None),
    )
    out_specs = P(("db", "batch"), "seq", None)
    return jax.shard_map(body, mesh=mesh, in_specs=in_specs, out_specs=out_specs, check_vma=False)
```

```python
import functools

import jax
import jax.numpy as jnp
from jax import lax
from jax.experimental import pallas as pl
from jax.experimental.pallas import tpu as pltpu
from jax.sharding import PartitionSpec as P

HEADS = 16
SPAN = 64
NBRS = 2
EPS = 1e-06
COLUMN = ("seq", "batch")
PLANE = ("db", "batch")
SIDE = 4
TILE = 512
NEAR = (1, 7, 2, 6)
FAR = (3, 5, 4)


def ring(value, axis, steps):
    count = lax.axis_size(axis)
    return lax.ppermute(value, axis, [(i, (i + steps) % count) for i in range(count)])


def shifted(place, along_x, steps):
    y, x = divmod(place, SIDE)
    return y * SIDE + (x + steps) % SIDE if along_x else (y + steps) % SIDE * SIDE + x


def plane_shift(value, stage, steps):
    pairs = []
    for place in range(lax.axis_size("db")):
        for core in range(lax.axis_size("batch")):
            goal = shifted(place, (core + stage) % 2 == 0, steps)
            pairs.append((place * 2 + core, goal * 2 + core))
    return lax.ppermute(value, PLANE, pairs)


def plane_gather(slab, later):
    first = {steps: plane_shift(slab, 0, steps) for steps in (1, 3, 2)}
    first = jnp.stack([slab] + [first[steps] for steps in (1, 2, 3)])
    first, later = lax.optimization_barrier((first, later))
    second = {steps: plane_shift(first, 1, steps) for steps in (1, 3, 2)}
    return [first] + [second[steps] for steps in (1, 2, 3)], later


def front_kernel(place_ref, gain_hbm_ref, database_ref, out_ref, raw_ref, gain_ref, sem, gain_sem):
    gain = pltpu.make_async_copy(gain_hbm_ref, gain_ref, gain_sem)
    gain.start()
    height = raw_ref.shape[1]
    start = pl.multiple_of(place_ref[3] * height, height)
    copy = pltpu.make_async_copy(database_ref.at[:, pl.ds(start, height)], raw_ref, sem)
    copy.start()
    gain.wait()
    copy.wait()
    raw = raw_ref[...].astype(jnp.float32)
    own = jnp.where(place_ref[2] == 0, raw[:, : height // 2], raw[:, height // 2 :])
    factor = lax.rsqrt(jnp.mean(own * own, axis=-1, keepdims=True) + EPS)
    out_ref[...] = (own * factor * gain_ref[...]).astype(jnp.bfloat16)


def front(place, gain, database, share):
    blocks, _, depth = database.shape
    hbm = pl.BlockSpec(memory_space=pltpu.HBM)
    gain, database = (pltpu.with_memory_space_constraint(a, pltpu.HBM) for a in (gain, database))
    return pl.pallas_call(
        front_kernel,
        out_shape=jax.ShapeDtypeStruct((blocks, share, depth), database.dtype),
        in_specs=[
            pl.BlockSpec(memory_space=pltpu.SMEM),
            hbm,
            hbm,
        ],
        out_specs=pl.BlockSpec(memory_space=pltpu.VMEM),
        scratch_shapes=[
            pltpu.VMEM((blocks, 2 * share, depth), database.dtype),
            pltpu.VMEM(gain.shape, gain.dtype),
            pltpu.SemaphoreType.DMA,
            pltpu.SemaphoreType.DMA,
        ],
        compiler_params=pltpu.CompilerParams(vmem_limit_bytes=4 * 2**20),
        name="front",
    )(place, gain, database)


def pick_kernel(place_ref, wanted_ref, *refs):
    pieces, outs, held_ref, sems = refs[:SIDE], refs[SIDE:-2], refs[-2], refs[-1]
    cores, slots = held_ref.shape[1:3]
    seq = len(outs)
    blocks = pieces[0].shape[0] // SIDE
    x, y, core, place = place_ref[0], place_ref[1], place_ref[2], place_ref[3]

    def one(code):
        shard, block = code >> blocks.bit_length() - 1, code & blocks - 1
        back_x = x - (shard & SIDE - 1) & SIDE - 1
        back_y = y - (shard >> SIDE.bit_length() - 1) & SIDE - 1
        inner = jnp.where(core == 0, back_x, back_y)
        outer = jnp.where(core == 0, back_y, back_x)
        where = inner * blocks + block
        value = pieces[0][where]
        for step in range(1, SIDE):
            value = jnp.where(outer == step, pieces[step][where], value)
        return value

    copies = [pltpu.make_async_copy(held_ref.at[k - 1], outs[k], sems.at[k - 1]) for k in range(1, seq)]
    for k in NEAR + FAR + (0,):
        goal_ref = held_ref.at[k - 1] if k else outs[0]
        for other in range(cores):
            side = core ^ other
            here = ((place + k & seq - 1) * cores + side) * slots
            before = ((place + k - 1 & seq - 1) * cores + side) * slots
            for slot in range(NBRS):
                goal_ref[other, slot] = one(wanted_ref[before + NBRS + slot])
                goal_ref[other, NBRS + slot] = one(wanted_ref[here + slot])
        if k:
            copies[k - 1].start()
    for copy in copies:
        copy.wait()


def pick(place, wanted, pieces, seq, cores, slots):
    smem = pl.BlockSpec(memory_space=pltpu.SMEM)
    shape = (cores, slots) + pieces[0].shape[1:]
    assert all(size & size - 1 == 0 for size in (SIDE, pieces[0].shape[0], seq, cores))
    return pl.pallas_call(
        pick_kernel,
        out_shape=[pltpu.VMEM(shape, pieces[0].dtype)]
        + [pltpu.HBM(shape, pieces[0].dtype)] * (seq - 1),
        in_specs=[smem, smem] + [pl.BlockSpec(memory_space=pltpu.VMEM)] * len(pieces),
        out_specs=[pl.BlockSpec(memory_space=pltpu.VMEM)]
        + [pl.BlockSpec(memory_space=pltpu.HBM)] * (seq - 1),
        scratch_shapes=[
            pltpu.VMEM((seq - 1,) + shape, pieces[0].dtype),
            pltpu.SemaphoreType.DMA((seq - 1,)),
        ],
        compiler_params=pltpu.CompilerParams(vmem_limit_bytes=8 * 2**20),
        name="pick",
    )(place, wanted, *pieces)


def pack_kernel(*refs):
    for part, ref in enumerate(refs[:-1]):
        refs[-1][part] = ref[1]


def pack(arrays):
    vmem = pl.BlockSpec(memory_space=pltpu.VMEM)
    return pl.pallas_call(
        pack_kernel,
        out_shape=jax.ShapeDtypeStruct((len(arrays),) + arrays[0].shape[1:], arrays[0].dtype),
        in_specs=[vmem] * len(arrays),
        out_specs=vmem,
        compiler_params=pltpu.CompilerParams(vmem_limit_bytes=4 * 2**20),
        name="pack",
    )(*arrays)


def column_rows(chosen, tile, behind):
    flat = lambda value: value.reshape(value.shape[0], -1, value.shape[-1])
    got = {k: ring(chosen[k], "seq", k) for k in NEAR}
    far = [chosen[k] for k in FAR]
    far, got[NEAR[0]] = lax.optimization_barrier((far, got[NEAR[0]]))
    got.update({k: ring(value, "seq", k) for k, value in zip(FAR, far)})
    behind, got[NEAR[1]] = lax.optimization_barrier((behind, got[NEAR[1]]))
    behind = ring(behind, "seq", 1)
    got[0] = chosen[0]
    order = (0,) + NEAR + FAR
    got, tile, behind = lax.optimization_barrier((got, tile, behind))
    other = lax.ppermute(pack([got[k] for k in order]), "batch", [(0, 1), (1, 0)])
    return [(flat(got[k]), 1) for k in order] + [(flat(other), len(order))], tile, behind


def bring_kernel(source_ref, out_ref, sem):
    copy = pltpu.make_async_copy(source_ref.at[0, :, pl.ds(0, out_ref.shape[1])], out_ref, sem)
    copy.start()
    copy.wait()


def bring(weight, columns):
    return pl.pallas_call(
        bring_kernel,
        out_shape=pltpu.VMEM((weight.shape[1], columns), weight.dtype),
        in_specs=[pl.BlockSpec(memory_space=pltpu.HBM)],
        out_specs=pl.BlockSpec(memory_space=pltpu.VMEM),
        scratch_shapes=[pltpu.SemaphoreType.DMA],
        compiler_params=pltpu.CompilerParams(vmem_limit_bytes=2**22),
        name="bring",
    )(pltpu.with_memory_space_constraint(weight, pltpu.HBM))


def prior_kernel(counts, *refs):
    tile_ref, weight_ref, query_ref, spare_ref, *rest = refs
    rows_refs, (out_ref, held_ref, *scratch, sems) = rest[:-8], rest[-8:]
    tiles = weight_ref.shape[2] // TILE
    early = tile_ref.shape[1] // TILE

    def load(piece):
        which, tile = divmod(piece, tiles)
        columns = pl.ds(tile * TILE, TILE)
        return pltpu.make_async_copy(
            weight_ref.at[which, :, columns], held_ref.at[piece - early], sems.at[piece - early]
        )

    for piece in range(early, 2 * tiles):
        load(piece).start()
    attend_kernel(
        counts, tile_ref, held_ref, query_ref, spare_ref, *rows_refs, out_ref, *scratch, span=0, load=load
    )


def attend_kernel(counts, *refs, span=1, load=None):
    tile_ref, held_ref, query_ref, spare_ref, *rest = refs
    rows_refs, rest = rest[:-6], rest[-6:]
    out_ref, normed_ref, keys_ref, values_ref, score_ref, share_ref = rest
    width = query_ref.shape[1]
    head = width // HEADS
    tiles = width // TILE
    early = tile_ref.shape[1] // TILE
    at = 0
    for rows_ref, parts in zip(rows_refs, counts):
        _, height, depth = rows_ref.shape
        share = height // 2
        size = parts * share
        rows = rows_ref[:parts, span * share : (span + 1) * share]
        normed_ref[at : at + size] = rows.reshape(size, depth)
        at += size

    def project(which, ref):
        for tile in range(tiles):
            columns = slice(tile * TILE, (tile + 1) * TILE)
            piece = which * tiles + tile
            if piece < early:
                weight = tile_ref[:, columns]
            else:
                if load is not None:
                    load(piece).wait()
                weight = held_ref[piece - early]
            product = jnp.dot(normed_ref[...], weight, preferred_element_type=jnp.float32)
            ref[:, columns] = product.astype(jnp.bfloat16)

    project(0, keys_ref)
    bottom = lax.broadcasted_iota(jnp.int32, (SPAN, head), 0) == SPAN - 1
    heads = [
        (slice(h * head, (h + 1) * head), slice(h * SPAN, (h + 1) * SPAN)) for h in range(HEADS)
    ]
    for columns, place in heads:
        queries = jnp.where(
            bottom,
            spare_ref[:, columns].astype(jnp.float32),
            query_ref[:, columns].astype(jnp.float32),
        ).astype(jnp.bfloat16)
        scores = lax.dot_general(
            queries, keys_ref[:, columns], (((1,), (1,)), ((), ())), preferred_element_type=jnp.float32
        )
        score_ref[place] = scores * head ** (-0.5)
    for columns, place in heads:
        scores = score_ref[place]
        raised = jnp.exp(scores - jnp.max(scores, axis=-1, keepdims=True))
        total = jnp.sum(raised, axis=-1, keepdims=True)
        share_ref[place] = (raised * (1.0 / total)).astype(jnp.bfloat16)
    project(1, values_ref)
    for columns, place in heads:
        mixed = jnp.dot(share_ref[place], values_ref[:, columns], preferred_element_type=jnp.float32)
        out_ref[:, columns] = mixed.astype(out_ref.dtype)


def attend(span, rows, weights, queries, spare):
    rows, counts = zip(*rows)
    _, height, depth = rows[0].shape
    tokens, width = queries.shape
    keys = sum(counts) * height // 2
    whole = pl.BlockSpec(memory_space=pltpu.VMEM)
    pieces = 2 * width // TILE - weights[0].shape[1] // TILE
    out_shape = [jax.ShapeDtypeStruct((SPAN, width), queries.dtype)]
    out_specs = [pl.BlockSpec((SPAN, width), lambda i: (0, 0))]
    scratch_shapes = [
        pltpu.VMEM((keys, depth), jnp.bfloat16),
        pltpu.VMEM((keys, width), jnp.bfloat16),
        pltpu.VMEM((keys, width), jnp.bfloat16),
        pltpu.VMEM((HEADS * SPAN, keys), jnp.float32),
        pltpu.VMEM((HEADS * SPAN, keys), jnp.bfloat16),
    ]
    if span == 0:
        weights = [weights[0], pltpu.with_memory_space_constraint(weights[1], pltpu.HBM)]
        out_shape.append(pltpu.VMEM((pieces, depth, TILE), queries.dtype))
        out_specs.append(whole)
        scratch_shapes.append(pltpu.SemaphoreType.DMA((pieces,)))
    flops = 4 * keys * depth * width
    return pl.pallas_call(
        functools.partial(prior_kernel if span == 0 else attend_kernel, counts),
        grid=(1,),
        out_shape=out_shape,
        in_specs=[
            whole,
            pl.BlockSpec(memory_space=pltpu.HBM) if span == 0 else whole,
            pl.BlockSpec((SPAN, width), lambda i: (span, 0)),
            whole,
            *[whole] * len(rows),
        ],
        out_specs=out_specs,
        scratch_shapes=scratch_shapes,
        compiler_params=pltpu.CompilerParams(vmem_limit_bytes=20 * 2**20),
        cost_estimate=pl.CostEstimate(flops=flops, bytes_accessed=2**20, transcendentals=2**18),
        name="attend",
    )(*weights, queries, spare, *rows)


def body(queries, database, enc_gain, kv_weight, shard_ids, block_ids):
    own = queries[0]
    tokens, width = own.shape
    blocks, height, depth = database.shape
    parts = lax.axis_size("seq") * lax.axis_size("batch")
    slots = 2 * NBRS
    share = height // parts
    shard = lax.axis_index("db")
    place = [shard % SIDE, shard // SIDE, lax.axis_index("batch"), lax.axis_index("seq")]
    place = jnp.stack(place).astype(jnp.int32)
    slab = front(place, enc_gain, database, share)
    wanted = shard_ids[..., 0] * blocks + block_ids
    wanted = jnp.broadcast_to(wanted, (parts,) + wanted.shape[1:])
    pieces, wanted = plane_gather(slab, wanted)
    wanted = lax.all_to_all(wanted, COLUMN, split_axis=0, concat_axis=0, tiled=True).reshape(-1)
    pieces = [piece.reshape(-1, share, depth) for piece in pieces]
    chosen = pick(place, wanted, pieces, lax.axis_size("seq"), lax.axis_size("batch"), slots)
    chosen, kv_weight = lax.optimization_barrier((chosen, kv_weight))
    tile = bring(kv_weight, TILE)
    rows, tile, last = column_rows(chosen, tile, own[tokens - 1 :])
    prior_out, held = attend(0, rows, [tile, kv_weight], own, last)
    back = ring(prior_out[SPAN - 1 :], "seq", -1)
    [own_out] = attend(1, rows, [tile, held], own, own[SPAN - 1 : SPAN])
    first = lax.axis_index("seq") == 0
    head = jnp.where(first, jnp.zeros_like(prior_out), prior_out)[: SPAN - 1]
    result = jnp.concatenate([head, own_out[SPAN - 1 :], own_out[: SPAN - 1], back])
    return result[None]


def solution(mesh):
    in_specs = (
        P(("db", "batch"), "seq", None),
        P("db", None, None),
        P(),
        P(),
        P(("db", "batch"), "seq", None, None),
        P(("db", "batch"), "seq", None),
    )
    out_specs = P(("db", "batch"), "seq", None)
    return jax.shard_map(body, mesh=mesh, in_specs=in_specs, out_specs=out_specs, check_vma=False)
```
